32 devices in a mesh: band: 4 (over y, core), tile: 8 (over z, x).
Axes of the slice: x: 2, y: 2, z: 4, core: 2. Of those that a mesh axis runs over, the one named last changes fastest.
Arguments:
- traces: float32 [64, 64, 1024], P(None, ('band', 'tile')), may hold values from -6 to 6
- bins: int32 [8], replicated, may hold values from 1 to 31, as said below
Outputs:
- dip_fields: float32 [8, 2, 64, 64, 128], P('band', None, 'tile')
The draws below stay inside these ranges and needn't reach their ends.
Inputs may be any that keep to these rules, and one draw needn't show every extreme that they name: 8 distinct bins, 1 and 31 among them.
All inputs are finite; a program needn't handle non-finite values.
Results may differ from the reference program's by a relative error of at most 0.00018.
Values sent between devices are 32-bit elements; how exact they have to be, the bound alone decides.
No kernel may reach another device: no remote copies, remote signals or barrier semaphores. Data moves between devices by JAX's collectives and lax.ppermute only.
A program may use at most 128 MiB of HBM per device.

```python
import math
import jax
import jax.numpy as jnp
from jax import lax

IL_DEV = 8
NT = 1024
NB = 8
WIN = 64
HOP = 8
SEG = 128
R = 3
NF = 128
IL = 64
XL = 64
N_TILE = 8


def draw_bins(key, part):
    inner = jax.random.permutation(key, WIN // 2 - 3)[:NB - 2].astype(jnp.int32) + 2
    return jnp.concatenate([jnp.array([1], jnp.int32), inner, jnp.array([WIN // 2 - 1], jnp.int32)])


def block_scale(rng, dims, cuts, smallest, top_value):
    def one(axis_at, parts):
        heights = jax.random.uniform(jax.random.fold_in(jax.random.fold_in(rng, 6), axis_at), (parts,), jnp.float32, smallest / len(cuts), top_value / len(cuts))
        return jnp.repeat(jnp.exp(heights), dims[axis_at] // parts).reshape((-1,) + (1,) * (len(dims) - axis_at - 1))

    factor_of = one(*cuts[0])
    for cut in cuts[1:]:
        factor_of = factor_of * one(*cut)
    return factor_of


def centred(stream_key, extent, spread, bound, cuts=(), kind=jnp.bfloat16):
    gain = block_scale(stream_key, extent, cuts, -0.22, 0.18) if cuts else 1.0
    drawn = jax.random.normal(stream_key, extent, jnp.float32) * spread * gain
    return jnp.minimum(jnp.maximum(drawn, -bound), bound).astype(kind)


def setup_inputs(seed: int = 0) -> dict:
    key_of = jax.random.split(jax.random.key(seed), 3)
    return {
        "traces": centred(key_of[0], (IL, XL, NT), 1.0, 6.0, ((1, 32),), jnp.float32),
        "bins": draw_bins(jax.random.fold_in(key_of[2], 71), 0),
    }


smooth_sigma = 2.0
tiny_value = 1e-06

def window_kernel(bins):
    band_count = bins.shape[0]
    sample_index = jnp.arange(WIN, dtype=jnp.int32)
    window_taper = 0.5 - 0.5 * jnp.cos(2.0 * math.pi / WIN * sample_index.astype(jnp.float32))
    phase_turns = bins[:, None] * sample_index[None, :] % WIN
    angles = 2.0 * math.pi / WIN * phase_turns.astype(jnp.float32)
    basis_rows = jnp.stack([window_taper * jnp.cos(angles), -window_taper * jnp.sin(angles)])
    frame_count = SEG // HOP
    seg_span = SEG + WIN - HOP
    offset = jnp.arange(seg_span, dtype=jnp.int32)[:, None] - HOP * jnp.arange(frame_count, dtype=jnp.int32)[None, :]
    inside = (offset >= 0) & (offset < WIN)
    picked = jnp.take(basis_rows, jnp.clip(offset, 0, WIN - 1), axis=2)
    kernel_table = jnp.where(inside[None, None], picked, 0.0)
    return jnp.transpose(kernel_table, (2, 0, 1, 3)).reshape(seg_span, 2 * band_count * frame_count)

def band_amplitude(traces, dft_kernel):
    frame_count = SEG // HOP
    seg_span = SEG + WIN - HOP
    block_count = NT // SEG
    band_count = dft_kernel.shape[1] // (2 * frame_count)
    padded = jnp.pad(traces, ((0, 0), (0, 0), (WIN // 2, WIN // 2)))
    pieces = jnp.stack([padded[:, :, block * SEG:block * SEG + seg_span] for block in range(block_count)], axis=2)
    spectra = jnp.dot(pieces, dft_kernel, precision=lax.Precision.HIGHEST, preferred_element_type=jnp.float32)
    spectra = spectra.reshape(traces.shape[0], traces.shape[1], block_count, 2, band_count, frame_count)
    real_part = spectra[:, :, :, 0]
    imag_part = spectra[:, :, :, 1]
    return jnp.sqrt(real_part * real_part + imag_part * imag_part)

def gradients(padded):
    grad_il = (padded[2:, 1:-1, 1:-1] - padded[:-2, 1:-1, 1:-1]) * 0.5
    grad_xl = (padded[1:-1, 2:, 1:-1] - padded[1:-1, :-2, 1:-1]) * 0.5
    grad_time = (padded[1:-1, 1:-1, 2:] - padded[1:-1, 1:-1, :-2]) * 0.5
    return (grad_il, grad_xl, grad_time)

def smooth_axis(field, axis, length):
    weights = [math.exp(-(offset_step * offset_step) / (2.0 * smooth_sigma * smooth_sigma)) for offset_step in range(-R, R + 1)]
    weight_sum = sum(weights)
    result = None
    for position, weight in enumerate(weights):
        section = lax.slice_in_dim(field, position, position + length, axis=axis)
        scaled = weight / weight_sum * section
        result = scaled if result is None else result + scaled
    return result

def smoothed_dips(grad_il, grad_xl, grad_time):
    width = grad_il.shape[0] - 2 * R
    stacked = jnp.stack([grad_il * grad_time, grad_xl * grad_time, grad_time * grad_time])
    along_rows = smooth_axis(stacked, 1, width)
    cross_pad = jnp.pad(along_rows, ((0, 0), (0, 0), (R, R), (0, 0)))
    along_cross = smooth_axis(cross_pad, 2, along_rows.shape[2])
    time_pad = jnp.pad(along_cross, ((0, 0), (0, 0), (0, 0), (R, R)))
    tensor = smooth_axis(time_pad, 3, along_rows.shape[3])
    denominator = tensor[2] + tiny_value
    return jnp.stack([-tensor[0] / denominator, -tensor[1] / denominator])

def band_dips(field):
    grad_il, grad_xl, grad_time = gradients(jnp.pad(field, 1))
    rim_pad = ((R, R), (0, 0), (0, 0))
    return smoothed_dips(jnp.pad(grad_il, rim_pad), jnp.pad(grad_xl, rim_pad), jnp.pad(grad_time, rim_pad))

def reference(traces, bins):
    dft_kernel = window_kernel(bins)
    by_tile = traces.reshape(N_TILE, IL_DEV, XL, NT)
    amplitude = lax.map(lambda block_rows: band_amplitude(block_rows, dft_kernel), by_tile)
    fields = jnp.transpose(amplitude, (4, 0, 1, 2, 3, 5)).reshape(NB, IL, XL, NF)
    return lax.map(band_dips, fields)
```

```python
import math

import jax
import jax.numpy as jnp
from jax import lax
from jax.experimental import pallas as pl
from jax.experimental.pallas import tpu as pltpu
from jax.sharding import PartitionSpec as P

NT = 1024
NB = 8
WIN = 64
HOP = 8
SEG = 128
R = 3
NF = 128
SUB = 8
RIM = R + 1

smooth_sigma = 2.0
tiny_value = 1e-06

VMEM_LIMIT = 48 * 1024 * 1024


def stencil_weights():
    weights = [math.exp(-(k * k) / (2.0 * smooth_sigma * smooth_sigma)) for k in range(-R, R + 1)]
    return [weight / sum(weights) for weight in weights]


def turn_sine(turns):
    shifted = (turns + WIN // 4) & (WIN - 1)
    folded = (shifted & (WIN // 2 - 1)) - WIN // 4
    angle = folded.astype(jnp.float32) * (2.0 * math.pi / WIN)
    square = angle * angle
    series = jnp.full_like(angle, -1.0 / 39916800.0)
    for coefficient in (1.0 / 362880.0, -1.0 / 5040.0, 1.0 / 120.0, -1.0 / 6.0, 1.0):
        series = series * square + coefficient
    value = series * angle
    return jnp.where(shifted >= WIN // 2, -value, value)


def turn_cosine(turns):
    return turn_sine(turns + WIN // 4)


def split_halves(value):
    high = value.astype(jnp.bfloat16)
    low = (value - high.astype(jnp.float32)).astype(jnp.bfloat16)
    return high, low


def fill_table(bins_ref, table_ref):
    frames = SEG // HOP
    lane = lax.broadcasted_iota(jnp.int32, (SUB, SEG), 1)
    row = lax.broadcasted_iota(jnp.int32, (SUB, SEG), 0)
    frame, band = lane % frames, lane // frames
    bin_of = jnp.zeros((SUB, SEG), jnp.int32)
    for b in range(NB):
        bin_of = jnp.where(band == b, bins_ref[b], bin_of)
    cosines, sines = [], []
    for group in range(WIN // SUB):
        sample = row + group * SUB
        taper = 0.5 - 0.5 * turn_cosine(sample)
        turns = (bin_of * sample) & (WIN - 1)
        cosines.append(taper * turn_cosine(turns))
        sines.append(-taper * turn_sine(turns))
    zero = jnp.zeros((SUB, SEG), jnp.float32)
    front = WIN // 2 // SUB
    body = SEG // SUB
    tail = (WIN // 2 - HOP) // SUB
    for part, basis in enumerate((cosines, sines)):
        columns = pl.ds(part * SEG, SEG)
        for group in range(front + body + tail):
            value = zero
            for piece in range(WIN // SUB):
                if 0 <= group - piece < frames:
                    value = jnp.where(frame == group - piece, basis[piece], value)
            if group < front:
                at = 2 * body - front + group
            else:
                at = group - front
            table_ref[pl.ds(at * SUB, SUB), columns] = value
        for at in range(body + tail, 2 * body - front):
            table_ref[pl.ds(at * SUB, SUB), columns] = zero


def swap_blocks_and_bands(tiles):
    frames = SEG // HOP
    lane = lax.broadcasted_iota(jnp.int32, (SUB, SEG), 1)
    tiles = list(tiles)
    step = NB // 2
    while step:
        upper = ((lane // frames) & step) != 0
        for at in range(NB):
            if at & step:
                continue
            first, second = tiles[at], tiles[at + step]
            tiles[at] = jnp.where(upper, pltpu.roll(second, frames * step, axis=1), first)
            tiles[at + step] = jnp.where(upper, second, pltpu.roll(first, SEG - frames * step, axis=1))
        step //= 2
    return tiles


def amplitude_kernel(n_band, n_tile, xl_part, bins_ref, x_ref, out_ref, table_ref):
    fill_table(bins_ref, table_ref)
    table_high, table_low = split_halves(table_ref[...])
    blocks = NT // SEG
    group_bands = NB // n_band
    pitch = blocks * xl_part
    lane = lax.broadcasted_iota(jnp.int32, (SUB, SEG), 1)
    from_next = lane < WIN // 2 - HOP
    from_last = lane >= SEG - WIN // 2
    zero = jnp.zeros((SUB, SEG), jnp.float32)
    blank = jnp.zeros((RIM, NF), jnp.float32)
    for tile in range(n_tile):
        own, near = [], []
        for xl in range(xl_part):
            line = [
                x_ref[pl.ds(tile * SUB * pitch + block * xl_part + xl, SUB, stride=pitch), :]
                for block in range(blocks)
            ]
            for block in range(blocks):
                later = line[block + 1] if block + 1 < blocks else zero
                earlier = line[block - 1] if block else zero
                near.append(jnp.where(from_next, later, jnp.where(from_last, earlier, zero)))
            own += line
        high, low = split_halves(
            jnp.concatenate([jnp.concatenate(own, 0), jnp.concatenate(near, 0)], 1)
        )
        spectra = jnp.dot(high, table_high, preferred_element_type=jnp.float32)
        spectra += jnp.dot(low, table_high, preferred_element_type=jnp.float32)
        spectra += jnp.dot(high, table_low, preferred_element_type=jnp.float32)
        real_part, imag_part = spectra[:, :SEG], spectra[:, SEG:]
        amplitude = jnp.sqrt(real_part * real_part + imag_part * imag_part)
        for xl in range(xl_part):
            rows = [
                amplitude[(xl * blocks + block) * SUB : (xl * blocks + block + 1) * SUB]
                for block in range(blocks)
            ]
            for band, field in enumerate(swap_blocks_and_bands(rows)):
                group, inner = band // group_bands, band % group_bands

                def place(at):
                    return ((group * n_tile + at) * group_bands + inner) * xl_part + xl

                out_ref[place(tile), RIM : RIM + SUB] = field
                if tile + 1 < n_tile:
                    out_ref[place(tile + 1), :RIM] = field[SUB - RIM :]
                else:
                    out_ref[place(tile), RIM + SUB :] = blank
                if tile:
                    out_ref[place(tile - 1), RIM + SUB :] = field[:RIM]
                else:
                    out_ref[place(tile), :RIM] = blank


def fill_smoother(smoother_ref):
    row = lax.broadcasted_iota(jnp.int32, (NF, NF), 0)
    column = lax.broadcasted_iota(jnp.int32, (NF, NF), 1)
    band_matrix = jnp.zeros((NF, NF), jnp.float32)
    for k, weight in zip(range(-R, R + 1), stencil_weights()):
        band_matrix = jnp.where(row - column == k, weight, band_matrix)
    high, low = split_halves(band_matrix)
    smoother_ref[:NF, :NF] = high
    smoother_ref[:NF, NF:] = low
    smoother_ref[NF:, :NF] = high
    smoother_ref[NF:, NF:] = jnp.zeros((NF, NF), jnp.bfloat16)


def weighted(taps, scale):
    weights = [weight * scale for weight in stencil_weights()]
    total = weights[R] * taps[R]
    for k in range(1, R + 1):
        total += weights[R + k] * (taps[R - k] + taps[R + k])
    return total


def dips_kernel(group_bands, xl_part, xl_all, chunk, e_ref, out_ref, product_ref, row_ref, smoother_ref):
    fill_smoother(smoother_ref)
    lane = lax.broadcasted_iota(jnp.int32, (SUB, NF), 1)
    at_first, at_last = lane == 0, lane == NF - 1
    zero = jnp.zeros((SUB, NF), jnp.float32)
    low_rows, high_rows = 1, 2 * RIM - 1

    for band in range(group_bands):
        for k in range(R):
            for field in range(3):
                row_ref[field, band, k] = zero
                row_ref[field, band, xl_all + R + k] = zero

    def place(band, xl):
        return (xl // xl_part) * (group_bands * xl_part) + band * xl_part + xl % xl_part

    def products(step, carry):
        for band in range(group_bands):
            for inner in range(chunk):
                xl = step * chunk + inner
                here = place(band, xl)
                before = place(band, jnp.maximum(xl - 1, 0))
                after = place(band, jnp.minimum(xl + 1, xl_all - 1))
                slot = band * chunk + inner
                for half, start in enumerate((low_rows, high_rows)):
                    value = e_ref[here, start : start + SUB]
                    grad_il = e_ref[here, start + 1 : start + 1 + SUB] - e_ref[here, start - 1 : start - 1 + SUB]
                    right = e_ref[after, start : start + SUB]
                    left = e_ref[before, start : start + SUB]
                    if inner == 0:
                        left = jnp.where(xl > 0, left, zero)
                    if inner == chunk - 1:
                        right = jnp.where(xl < xl_all - 1, right, zero)
                    grad_xl = right - left
                    grad_time = jnp.where(at_last, zero, pltpu.roll(value, NF - 1, axis=1)) - jnp.where(
                        at_first, zero, pltpu.roll(value, 1, axis=1)
                    )
                    rows = slice(start - low_rows, start - low_rows + SUB)
                    product_ref[0, slot, rows] = grad_il * grad_time
                    product_ref[1, slot, rows] = grad_xl * grad_time
                    product_ref[2, slot, rows] = grad_time * grad_time
                for field in range(3):
                    taps = [product_ref[field, slot, k : k + SUB] for k in range(2 * R + 1)]
                    row_ref[field, band, xl + R] = weighted(taps, 0.25)
        return carry

    lax.fori_loop(0, xl_all // chunk, products, 0)

    def smooth(step, carry):
        for band in range(group_bands):
            fields = []
            for field in range(3):
                for inner in range(chunk):
                    xl = step * chunk + inner
                    fields.append(weighted([row_ref[field, band, xl + k] for k in range(2 * R + 1)], 1.0))
            high, low = split_halves(jnp.concatenate(fields, 0))
            both = jnp.concatenate([high, low], 1)
            tensor = jnp.dot(both, smoother_ref[...], preferred_element_type=jnp.float32)
            tensor = tensor[:, :NF] + tensor[:, NF:]
            size = chunk * SUB
            inverse = -1.0 / (tensor[2 * size :] + tiny_value)
            for field in range(2):
                dip = tensor[field * size : (field + 1) * size] * inverse
                for inner in range(chunk):
                    base = (band * 2 + field) * SUB * xl_all + step * chunk + inner
                    out_ref[pl.ds(base, SUB, stride=xl_all), :] = dip[inner * SUB : (inner + 1) * SUB]
        return carry

    lax.fori_loop(0, xl_all // chunk, smooth, 0)


def local(traces, bins):
    n_band = lax.axis_size("band")
    n_tile = lax.axis_size("tile")
    il_all, xl_part, _ = traces.shape
    tile_rows = il_all // n_tile
    group_bands = NB // n_band
    devices = n_band * n_tile
    xl_all = devices * xl_part
    blocks = NT // SEG
    window = tile_rows + 2 * RIM
    chunk = 8

    lines = traces.reshape(il_all, xl_part, blocks, SEG)
    lines = jnp.transpose(lines, (0, 2, 1, 3)).reshape(il_all * blocks * xl_part, SEG)
    vmem = pl.BlockSpec(memory_space=pltpu.VMEM)
    payload = pl.pallas_call(
        lambda *refs: amplitude_kernel(n_band, n_tile, xl_part, *refs),
        out_shape=jax.ShapeDtypeStruct((devices * group_bands * xl_part, window, NF), jnp.float32),
        in_specs=[pl.BlockSpec(memory_space=pltpu.SMEM), vmem],
        out_specs=vmem,
        scratch_shapes=[pltpu.VMEM((2 * SEG, 2 * SEG), jnp.float32)],
        compiler_params=pltpu.CompilerParams(vmem_limit_bytes=VMEM_LIMIT),
        name="amplitudes",
    )(bins, lines)
    payload = payload.reshape(devices, group_bands * xl_part, window, NF)
    bricks = lax.all_to_all(payload, ("band", "tile"), split_axis=0, concat_axis=0, tiled=True)
    dips = pl.pallas_call(
        lambda *refs: dips_kernel(group_bands, xl_part, xl_all, chunk, *refs),
        out_shape=jax.ShapeDtypeStruct((group_bands * 2 * tile_rows * xl_all, NF), jnp.float32),
        in_specs=[vmem],
        out_specs=vmem,
        scratch_shapes=[
            pltpu.VMEM((3, group_bands * chunk, 2 * RIM + SUB, NF), jnp.float32),
            pltpu.VMEM((3, group_bands, xl_all + 2 * R, SUB, NF), jnp.float32),
            pltpu.VMEM((2 * NF, 2 * NF), jnp.bfloat16),
        ],
        compiler_params=pltpu.CompilerParams(vmem_limit_bytes=VMEM_LIMIT),
        name="dips",
    )(bricks.reshape(devices * group_bands * xl_part, window, NF))
    return dips.reshape(group_bands, 2, tile_rows, xl_all, NF)


def solution(mesh):
    in_specs = (P(None, ("band", "tile"), None), P())
    out_specs = P("band", None, "tile", None, None)
    return jax.shard_map(local, mesh=mesh, in_specs=in_specs, out_specs=out_specs, check_vma=False)
```

```python
import math

import jax
import jax.numpy as jnp
from jax import lax
from jax.experimental import pallas as pl
from jax.experimental.pallas import tpu as pltpu
from jax.sharding import PartitionSpec as P

NT = 1024
NB = 8
WIN = 64
HOP = 8
SEG = 128
R = 3
NF = 128
SUB = 8
RIM = R + 1

smooth_sigma = 2.0
tiny_value = 1e-06

VMEM_LIMIT = 48 * 1024 * 1024


def stencil_weights():
    weights = [math.exp(-(k * k) / (2.0 * smooth_sigma * smooth_sigma)) for k in range(-R, R + 1)]
    return [weight / sum(weights) for weight in weights]


def turn_sine(turns):
    shifted = (turns + WIN // 4) & (WIN - 1)
    folded = (shifted & (WIN // 2 - 1)) - WIN // 4
    angle = folded.astype(jnp.float32) * (2.0 * math.pi / WIN)
    square = angle * angle
    series = jnp.full_like(angle, -1.0 / 39916800.0)
    for coefficient in (1.0 / 362880.0, -1.0 / 5040.0, 1.0 / 120.0, -1.0 / 6.0, 1.0):
        series = series * square + coefficient
    value = series * angle
    return jnp.where(shifted >= WIN // 2, -value, value)


def turn_cosine(turns):
    return turn_sine(turns + WIN // 4)


def split_halves(value):
    high = value.astype(jnp.bfloat16)
    low = (value - high.astype(jnp.float32)).astype(jnp.bfloat16)
    return high, low


def fill_table(bins_ref, table_ref):
    frames = SEG // HOP
    lane = lax.broadcasted_iota(jnp.int32, (SUB, SEG), 1)
    row = lax.broadcasted_iota(jnp.int32, (SUB, SEG), 0)
    frame, band = lane % frames, lane // frames
    bin_of = jnp.zeros((SUB, SEG), jnp.int32)
    for b in range(NB):
        bin_of = jnp.where(band == b, bins_ref[b], bin_of)
    cosines, sines = [], []
    for group in range(WIN // SUB):
        sample = row + group * SUB
        taper = 0.5 - 0.5 * turn_cosine(sample)
        turns = (bin_of * sample) & (WIN - 1)
        cosines.append(taper * turn_cosine(turns))
        sines.append(-taper * turn_sine(turns))
    zero = jnp.zeros((SUB, SEG), jnp.float32)
    front = WIN // 2 // SUB
    body = SEG // SUB
    tail = (WIN // 2 - HOP) // SUB
    for part, basis in enumerate((cosines, sines)):
        columns = pl.ds(part * SEG, SEG)
        for group in range(front + body + tail):
            value = zero
            for piece in range(WIN // SUB):
                if 0 <= group - piece < frames:
                    value = jnp.where(frame == group - piece, basis[piece], value)
            if group < front:
                at = 2 * body - front + group
            else:
                at = group - front
            table_ref[pl.ds(at * SUB, SUB), columns] = value
        for at in range(body + tail, 2 * body - front):
            table_ref[pl.ds(at * SUB, SUB), columns] = zero


def swap_blocks_and_bands(tiles):
    frames = SEG // HOP
    lane = lax.broadcasted_iota(jnp.int32, (SUB, SEG), 1)
    tiles = list(tiles)
    step = NB // 2
    while step:
        upper = ((lane // frames) & step) != 0
        for at in range(NB):
            if at & step:
                continue
            first, second = tiles[at], tiles[at + step]
            tiles[at] = jnp.where(upper, pltpu.roll(second, frames * step, axis=1), first)
            tiles[at + step] = jnp.where(upper, second, pltpu.roll(first, SEG - frames * step, axis=1))
        step //= 2
    return tiles


def amplitude_kernel(
    n_band, n_tile, xl_part, far_bins_ref, far_ref, out_ref, table_ref, bins_ref, x_ref, bins_sem, x_sem
):
    bins_copy = pltpu.make_async_copy(far_bins_ref, bins_ref, bins_sem)
    bins_copy.start()
    x_copy = pltpu.make_async_copy(far_ref, x_ref, x_sem)
    x_copy.start()
    bins_copy.wait()
    fill_table(bins_ref, table_ref)
    x_copy.wait()
    table_high, table_low = split_halves(table_ref[...])
    blocks = NT // SEG
    group_bands = NB // n_band
    pitch = blocks * xl_part
    lane = lax.broadcasted_iota(jnp.int32, (SUB, SEG), 1)
    from_next = lane < WIN // 2 - HOP
    from_last = lane >= SEG - WIN // 2
    zero = jnp.zeros((SUB, SEG), jnp.float32)
    blank = jnp.zeros((RIM, NF), jnp.float32)
    for tile in range(n_tile):
        own, near = [], []
        for xl in range(xl_part):
            line = [
                x_ref[pl.ds(tile * SUB * pitch + block * xl_part + xl, SUB, stride=pitch), :]
                for block in range(blocks)
            ]
            for block in range(blocks):
                later = line[block + 1] if block + 1 < blocks else zero
                earlier = line[block - 1] if block else zero
                near.append(jnp.where(from_next, later, jnp.where(from_last, earlier, zero)))
            own += line
        high, low = split_halves(
            jnp.concatenate([jnp.concatenate(own, 0), jnp.concatenate(near, 0)], 1)
        )
        spectra = jnp.dot(high, table_high, preferred_element_type=jnp.float32)
        spectra += jnp.dot(low, table_high, preferred_element_type=jnp.float32)
        spectra += jnp.dot(high, table_low, preferred_element_type=jnp.float32)
        real_part, imag_part = spectra[:, :SEG], spectra[:, SEG:]
        amplitude = jnp.sqrt(real_part * real_part + imag_part * imag_part)
        for xl in range(xl_part):
            rows = [
                amplitude[(xl * blocks + block) * SUB : (xl * blocks + block + 1) * SUB]
                for block in range(blocks)
            ]
            for band, field in enumerate(swap_blocks_and_bands(rows)):
                group, inner = band // group_bands, band % group_bands

                def place(at):
                    return ((group * n_tile + at) * group_bands + inner) * xl_part + xl

                out_ref[place(tile), RIM : RIM + SUB] = field
                if tile + 1 < n_tile:
                    out_ref[place(tile + 1), :RIM] = field[SUB - RIM :]
                else:
                    out_ref[place(tile), RIM + SUB :] = blank
                if tile:
                    out_ref[place(tile - 1), RIM + SUB :] = field[:RIM]
                else:
                    out_ref[place(tile), :RIM] = blank


def fill_smoother(smoother_ref):
    row = lax.broadcasted_iota(jnp.int32, (NF, NF), 0)
    column = lax.broadcasted_iota(jnp.int32, (NF, NF), 1)
    band_matrix = jnp.zeros((NF, NF), jnp.float32)
    for k, weight in zip(range(-R, R + 1), stencil_weights()):
        band_matrix = jnp.where(row - column == k, weight, band_matrix)
    high, low = split_halves(band_matrix)
    smoother_ref[:NF, :NF] = high
    smoother_ref[:NF, NF:] = low
    smoother_ref[NF:, :NF] = high
    smoother_ref[NF:, NF:] = jnp.zeros((NF, NF), jnp.bfloat16)


def weighted(taps, scale):
    weights = [weight * scale for weight in stencil_weights()]
    total = weights[R] * taps[R]
    for k in range(1, R + 1):
        total += weights[R + k] * (taps[R - k] + taps[R + k])
    return total


def dips_kernel(
    group_bands, xl_part, xl_all, chunk, e_ref, out_ref, stage_ref, product_ref, row_ref, smoother_ref, sent_ref
):
    fill_smoother(smoother_ref)
    lane = lax.broadcasted_iota(jnp.int32, (SUB, NF), 1)
    at_first, at_last = lane == 0, lane == NF - 1
    zero = jnp.zeros((SUB, NF), jnp.float32)
    low_rows, high_rows = 1, 2 * RIM - 1

    for band in range(group_bands):
        for k in range(R):
            for field in range(3):
                row_ref[field, band, k] = zero
                row_ref[field, band, xl_all + R + k] = zero

    def place(band, xl):
        return (xl // xl_part) * (group_bands * xl_part) + band * xl_part + xl % xl_part

    def shifted_time(value):
        later = jnp.where(at_last, zero, pltpu.roll(value, NF - 1, axis=1))
        return later - jnp.where(at_first, zero, pltpu.roll(value, 1, axis=1))

    def products(band, first):
        lines = []
        for xl in range(first - 1, first + chunk + 1):
            if 0 <= xl < xl_all:
                lines.append([e_ref[place(band, xl), s : s + SUB] for s in (low_rows, high_rows)])
            else:
                lines.append([zero, zero])
        for inner in range(chunk):
            xl = first + inner
            here = place(band, xl)
            slot = xl % (2 * chunk)
            for half, start in enumerate((low_rows, high_rows)):
                value = lines[inner + 1][half]
                grad_il = e_ref[here, start + 1 : start + 1 + SUB] - e_ref[here, start - 1 : start - 1 + SUB]
                grad_xl = lines[inner + 2][half] - lines[inner][half]
                grad_time = shifted_time(value)
                rows = slice(start - low_rows, start - low_rows + SUB)
                product_ref[0, slot, rows] = grad_il * grad_time
                product_ref[1, slot, rows] = grad_xl * grad_time
                product_ref[2, slot, rows] = grad_time * grad_time
            for field in range(3):
                taps = [product_ref[field, slot, k : k + SUB] for k in range(2 * R + 1)]
                row_ref[field, band, xl + R] = weighted(taps, 0.25)

    def smooth(band, first):
        slot = band * (xl_all // chunk) + first // chunk
        fields = []
        for field in range(3):
            taps = [row_ref[field, band, first + k] for k in range(chunk + 2 * R)]
            for inner in range(chunk):
                fields.append(weighted(taps[inner : inner + 2 * R + 1], 1.0))
        high, low = split_halves(jnp.concatenate(fields, 0))
        both = jnp.concatenate([high, low], 1)
        tensor = jnp.dot(both, smoother_ref[...], preferred_element_type=jnp.float32)
        tensor = tensor[:, :NF] + tensor[:, NF:]
        size = chunk * SUB
        inverse = -1.0 / (tensor[2 * size :] + tiny_value)
        for field in range(2):
            dip = tensor[field * size : (field + 1) * size] * inverse
            for inner in range(chunk):
                rows = pl.ds(field * SUB * chunk + inner, SUB, stride=chunk)
                stage_ref[slot, rows, :] = dip[inner * SUB : (inner + 1) * SUB]
        copies = []
        for at in range(2 * SUB):
            copies.append(pltpu.make_async_copy(
                stage_ref.at[slot, pl.ds(at * chunk, chunk)],
                out_ref.at[pl.ds((band * 2 * SUB + at) * xl_all + first, chunk)],
                sent_ref.at[slot],
            ))
            copies[-1].start()
        return copies

    copies = []
    for band in range(group_bands):
        for first in range(0, xl_all, chunk):
            products(band, first)
            if first:
                copies += smooth(band, first - chunk)
        copies += smooth(band, xl_all - chunk)
    for copy in copies:
        copy.wait()


def local(traces, bins):
    n_band = lax.axis_size("band")
    n_tile = lax.axis_size("tile")
    il_all, xl_part, _ = traces.shape
    tile_rows = il_all // n_tile
    group_bands = NB // n_band
    devices = n_band * n_tile
    xl_all = devices * xl_part
    blocks = NT // SEG
    window = tile_rows + 2 * RIM
    chunk = 8

    lines = traces.reshape(il_all, xl_part, blocks, SEG)
    lines = jnp.transpose(lines, (0, 2, 1, 3)).reshape(il_all * blocks * xl_part, SEG)
    vmem = pl.BlockSpec(memory_space=pltpu.VMEM)
    payload = pl.pallas_call(
        lambda *refs: amplitude_kernel(n_band, n_tile, xl_part, *refs),
        out_shape=jax.ShapeDtypeStruct((devices * group_bands * xl_part, window, NF), jnp.float32),
        in_specs=[pl.BlockSpec(memory_space=pltpu.HBM)] * 2,
        out_specs=vmem,
        scratch_shapes=[
            pltpu.VMEM((2 * SEG, 2 * SEG), jnp.float32),
            pltpu.SMEM(bins.shape, jnp.int32),
            pltpu.VMEM(lines.shape, jnp.float32),
            pltpu.SemaphoreType.DMA,
            pltpu.SemaphoreType.DMA,
        ],
        compiler_params=pltpu.CompilerParams(vmem_limit_bytes=VMEM_LIMIT),
        name="amplitudes",
    )(pltpu.with_memory_space_constraint(bins, pltpu.HBM), pltpu.with_memory_space_constraint(lines, pltpu.HBM))
    payload = payload.reshape(devices, group_bands * xl_part, window, NF)
    bricks = lax.all_to_all(payload, ("band", "tile"), split_axis=0, concat_axis=0, tiled=True)
    steps = group_bands * xl_all // chunk
    dips = pl.pallas_call(
        lambda *refs: dips_kernel(group_bands, xl_part, xl_all, chunk, *refs),
        out_shape=jax.ShapeDtypeStruct((group_bands * 2 * tile_rows * xl_all, NF), jnp.float32),
        in_specs=[vmem],
        out_specs=pl.BlockSpec(memory_space=pltpu.HBM),
        scratch_shapes=[
            pltpu.VMEM((steps, 2 * SUB * chunk, NF), jnp.float32),
            pltpu.VMEM((3, 2 * chunk, 2 * RIM + SUB, NF), jnp.float32),
            pltpu.VMEM((3, group_bands, xl_all + 2 * R, SUB, NF), jnp.float32),
            pltpu.VMEM((2 * NF, 2 * NF), jnp.bfloat16),
            pltpu.SemaphoreType.DMA((steps,)),
        ],
        compiler_params=pltpu.CompilerParams(vmem_limit_bytes=VMEM_LIMIT),
        name="dips",
    )(bricks.reshape(devices * group_bands * xl_part, window, NF))
    return dips.reshape(group_bands, 2, tile_rows, xl_all, NF)


def solution(mesh):
    in_specs = (P(None, ("band", "tile"), None), P())
    out_specs = P("band", None, "tile", None, None)
    return jax.shard_map(local, mesh=mesh, in_specs=in_specs, out_specs=out_specs, check_vma=False)
```

```python
import math

import jax
import jax.numpy as jnp
from jax import lax
from jax.experimental import pallas as pl
from jax.experimental.pallas import tpu as pltpu
from jax.sharding import PartitionSpec as P

NT = 1024
NB = 8
WIN = 64
HOP = 8
SEG = 128
R = 3
NF = 128
SUB = 8
RIM = R + 1

smooth_sigma = 2.0
tiny_value = 1e-06

VMEM_LIMIT = 48 * 1024 * 1024


def stencil_weights():
    weights = [math.exp(-(k * k) / (2.0 * smooth_sigma * smooth_sigma)) for k in range(-R, R + 1)]
    return [weight / sum(weights) for weight in weights]


def turn_sine(turns):
    shifted = (turns + WIN // 4) & (WIN - 1)
    folded = (shifted & (WIN // 2 - 1)) - WIN // 4
    angle = folded.astype(jnp.float32) * (2.0 * math.pi / WIN)
    square = angle * angle
    series = jnp.full_like(angle, -1.0 / 39916800.0)
    for coefficient in (1.0 / 362880.0, -1.0 / 5040.0, 1.0 / 120.0, -1.0 / 6.0, 1.0):
        series = series * square + coefficient
    value = series * angle
    return jnp.where(shifted >= WIN // 2, -value, value)


def turn_cosine(turns):
    return turn_sine(turns + WIN // 4)


def split_halves(value):
    high = value.astype(jnp.bfloat16)
    low = (value - high.astype(jnp.float32)).astype(jnp.bfloat16)
    return high, low


def fill_table(bins_ref, table_ref):
    frames = SEG // HOP
    lane = lax.broadcasted_iota(jnp.int32, (SUB, SEG), 1)
    row = lax.broadcasted_iota(jnp.int32, (SUB, SEG), 0)
    frame, band = lane % frames, lane // frames
    bin_of = jnp.zeros((SUB, SEG), jnp.int32)
    for b in range(NB):
        bin_of = jnp.where(band == b, bins_ref[b], bin_of)
    cosines, sines = [], []
    for group in range(WIN // SUB):
        sample = row + group * SUB
        taper = 0.5 - 0.5 * turn_cosine(sample)
        turns = (bin_of * sample) & (WIN - 1)
        cosines.append(taper * turn_cosine(turns))
        sines.append(-taper * turn_sine(turns))
    zero = jnp.zeros((SUB, SEG), jnp.float32)
    front = WIN // 2 // SUB
    body = SEG // SUB
    tail = (WIN // 2 - HOP) // SUB
    for part, basis in enumerate((cosines, sines)):
        columns = pl.ds(part * SEG, SEG)
        for group in range(front + body + tail):
            value = zero
            for piece in range(WIN // SUB):
                if 0 <= group - piece < frames:
                    value = jnp.where(frame == group - piece, basis[piece], value)
            if group < front:
                at = 2 * body - front + group
            else:
                at = group - front
            table_ref[pl.ds(at * SUB, SUB), columns] = value
        for at in range(body + tail, 2 * body - front):
            table_ref[pl.ds(at * SUB, SUB), columns] = zero


def swap_blocks_and_bands(tiles):
    frames = SEG // HOP
    lane = lax.broadcasted_iota(jnp.int32, (SUB, SEG), 1)
    tiles = list(tiles)
    step = NB // 2
    while step:
        upper = ((lane // frames) & step) != 0
        for at in range(NB):
            if at & step:
                continue
            first, second = tiles[at], tiles[at + step]
            tiles[at] = jnp.where(upper, pltpu.roll(second, frames * step, axis=1), first)
            tiles[at + step] = jnp.where(upper, second, pltpu.roll(first, SEG - frames * step, axis=1))
        step //= 2
    return tiles


def exchange_order(n_band, n_tile):
    order = []
    for step in range(2 * n_band):
        last, band = divmod(step ^ (step >> 1), n_band)
        order += [band * n_tile + tile for tile in range(last, n_tile, 2)]
    return order


def amplitude_kernel(
    n_band, n_tile, xl_part, far_bins_ref, far_ref, out_ref, table_ref, bins_ref, x_ref, bins_sem, x_sem
):
    bins_copy = pltpu.make_async_copy(far_bins_ref, bins_ref, bins_sem)
    bins_copy.start()
    x_copy = pltpu.make_async_copy(far_ref, x_ref, x_sem)
    x_copy.start()
    bins_copy.wait()
    fill_table(bins_ref, table_ref)
    x_copy.wait()
    table_high, table_low = split_halves(table_ref[...])
    blocks = NT // SEG
    group_bands = NB // n_band
    order = exchange_order(n_band, n_tile)
    pitch = blocks * xl_part
    lane = lax.broadcasted_iota(jnp.int32, (SUB, SEG), 1)
    from_next = lane < WIN // 2 - HOP
    from_last = lane >= SEG - WIN // 2
    zero = jnp.zeros((SUB, SEG), jnp.float32)
    blank = jnp.zeros((RIM, NF), jnp.float32)
    for tile in range(n_tile):
        own, near = [], []
        for xl in range(xl_part):
            line = [
                x_ref[pl.ds(tile * SUB * pitch + block * xl_part + xl, SUB, stride=pitch), :]
                for block in range(blocks)
            ]
            for block in range(blocks):
                later = line[block + 1] if block + 1 < blocks else zero
                earlier = line[block - 1] if block else zero
                near.append(jnp.where(from_next, later, jnp.where(from_last, earlier, zero)))
            own += line
        high, low = split_halves(
            jnp.concatenate([jnp.concatenate(own, 0), jnp.concatenate(near, 0)], 1)
        )
        spectra = jnp.dot(high, table_high, preferred_element_type=jnp.float32)
        spectra += jnp.dot(low, table_high, preferred_element_type=jnp.float32)
        spectra += jnp.dot(high, table_low, preferred_element_type=jnp.float32)
        real_part, imag_part = spectra[:, :SEG], spectra[:, SEG:]
        amplitude = jnp.sqrt(real_part * real_part + imag_part * imag_part)
        for xl in range(xl_part):
            rows = [
                amplitude[(xl * blocks + block) * SUB : (xl * blocks + block + 1) * SUB]
                for block in range(blocks)
            ]
            for band, field in enumerate(swap_blocks_and_bands(rows)):
                group, inner = band // group_bands, band % group_bands

                def place(at):
                    return (order.index(group * n_tile + at) * group_bands + inner) * xl_part + xl

                out_ref[place(tile), RIM : RIM + SUB] = field
                if tile + 1 < n_tile:
                    out_ref[place(tile + 1), :RIM] = field[SUB - RIM :]
                else:
                    out_ref[place(tile), RIM + SUB :] = blank
                if tile:
                    out_ref[place(tile - 1), RIM + SUB :] = field[:RIM]
                else:
                    out_ref[place(tile), :RIM] = blank


def fill_smoother(smoother_ref):
    row = lax.broadcasted_iota(jnp.int32, (NF, NF), 0)
    column = lax.broadcasted_iota(jnp.int32, (NF, NF), 1)
    band_matrix = jnp.zeros((NF, NF), jnp.float32)
    for k, weight in zip(range(-R, R + 1), stencil_weights()):
        band_matrix = jnp.where(row - column == k, weight, band_matrix)
    high, low = split_halves(band_matrix)
    smoother_ref[:NF, :NF] = high
    smoother_ref[:NF, NF:] = low
    smoother_ref[NF:, :NF] = high
    smoother_ref[NF:, NF:] = jnp.zeros((NF, NF), jnp.bfloat16)


def weighted(taps, scale):
    weights = [weight * scale for weight in stencil_weights()]
    total = weights[R] * taps[R]
    for k in range(1, R + 1):
        total += weights[R + k] * (taps[R - k] + taps[R + k])
    return total


def dips_kernel(
    order, group_bands, xl_part, xl_all, chunk, e_ref, out_ref, stage_ref, product_ref, row_ref, smoother_ref, sent_ref
):
    fill_smoother(smoother_ref)
    lane = lax.broadcasted_iota(jnp.int32, (SUB, NF), 1)
    at_first, at_last = lane == 0, lane == NF - 1
    zero = jnp.zeros((SUB, NF), jnp.float32)
    low_rows, high_rows = 1, 2 * RIM - 1

    for band in range(group_bands):
        for k in range(R):
            for field in range(3):
                row_ref[field, band, k] = zero
                row_ref[field, band, xl_all + R + k] = zero

    def place(band, xl):
        return order.index(xl // xl_part) * (group_bands * xl_part) + band * xl_part + xl % xl_part

    def shifted_time(value):
        later = jnp.where(at_last, zero, pltpu.roll(value, NF - 1, axis=1))
        return later - jnp.where(at_first, zero, pltpu.roll(value, 1, axis=1))

    def products(band, first):
        lines = []
        for xl in range(first - 1, first + chunk + 1):
            if 0 <= xl < xl_all:
                lines.append([e_ref[place(band, xl), s : s + SUB] for s in (low_rows, high_rows)])
            else:
                lines.append([zero, zero])
        for inner in range(chunk):
            xl = first + inner
            here = place(band, xl)
            slot = xl % (2 * chunk)
            for half, start in enumerate((low_rows, high_rows)):
                value = lines[inner + 1][half]
                grad_il = e_ref[here, start + 1 : start + 1 + SUB] - e_ref[here, start - 1 : start - 1 + SUB]
                grad_xl = lines[inner + 2][half] - lines[inner][half]
                grad_time = shifted_time(value)
                rows = slice(start - low_rows, start - low_rows + SUB)
                product_ref[0, slot, rows] = grad_il * grad_time
                product_ref[1, slot, rows] = grad_xl * grad_time
                product_ref[2, slot, rows] = grad_time * grad_time
            for field in range(3):
                taps = [product_ref[field, slot, k : k + SUB] for k in range(2 * R + 1)]
                row_ref[field, band, xl + R] = weighted(taps, 0.25)

    def smooth(band, first):
        slot = band * (xl_all // chunk) + first // chunk
        fields = []
        for field in range(3):
            taps = [row_ref[field, band, first + k] for k in range(chunk + 2 * R)]
            for inner in range(chunk):
                fields.append(weighted(taps[inner : inner + 2 * R + 1], 1.0))
        high, low = split_halves(jnp.concatenate(fields, 0))
        both = jnp.concatenate([high, low], 1)
        tensor = jnp.dot(both, smoother_ref[...], preferred_element_type=jnp.float32)
        tensor = tensor[:, :NF] + tensor[:, NF:]
        size = chunk * SUB
        inverse = -1.0 / (tensor[2 * size :] + tiny_value)
        for field in range(2):
            dip = tensor[field * size : (field + 1) * size] * inverse
            for inner in range(chunk):
                rows = pl.ds(field * SUB * chunk + inner, SUB, stride=chunk)
                stage_ref[slot, rows, :] = dip[inner * SUB : (inner + 1) * SUB]
        copies = []
        for at in range(2 * SUB):
            copies.append(pltpu.make_async_copy(
                stage_ref.at[slot, pl.ds(at * chunk, chunk)],
                out_ref.at[pl.ds((band * 2 * SUB + at) * xl_all + first, chunk)],
                sent_ref.at[slot],
            ))
            copies[-1].start()
        return copies

    copies = []
    for band in range(group_bands):
        for first in range(0, xl_all, chunk):
            products(band, first)
            if first:
                copies += smooth(band, first - chunk)
        copies += smooth(band, xl_all - chunk)
    for copy in copies:
        copy.wait()


def local(traces, bins):
    n_band = lax.axis_size("band")
    n_tile = lax.axis_size("tile")
    il_all, xl_part, _ = traces.shape
    tile_rows = il_all // n_tile
    group_bands = NB // n_band
    devices = n_band * n_tile
    order = exchange_order(n_band, n_tile)
    xl_all = devices * xl_part
    blocks = NT // SEG
    window = tile_rows + 2 * RIM
    chunk = 8

    lines = traces.reshape(il_all, xl_part, blocks, SEG)
    lines = jnp.transpose(lines, (0, 2, 1, 3)).reshape(il_all * blocks * xl_part, SEG)
    vmem = pl.BlockSpec(memory_space=pltpu.VMEM)
    payload = pl.pallas_call(
        lambda *refs: amplitude_kernel(n_band, n_tile, xl_part, *refs),
        out_shape=jax.ShapeDtypeStruct((devices * group_bands * xl_part, window, NF), jnp.float32),
        in_specs=[pl.BlockSpec(memory_space=pltpu.HBM)] * 2,
        out_specs=vmem,
        scratch_shapes=[
            pltpu.VMEM((2 * SEG, 2 * SEG), jnp.float32),
            pltpu.SMEM(bins.shape, jnp.int32),
            pltpu.VMEM(lines.shape, jnp.float32),
            pltpu.SemaphoreType.DMA,
            pltpu.SemaphoreType.DMA,
        ],
        compiler_params=pltpu.CompilerParams(vmem_limit_bytes=VMEM_LIMIT),
        name="amplitudes",
    )(pltpu.with_memory_space_constraint(bins, pltpu.HBM), pltpu.with_memory_space_constraint(lines, pltpu.HBM))
    payload = payload.reshape(devices, group_bands * xl_part, window, NF)
    bricks = lax.all_to_all(
        payload, ("band", "tile"), split_axis=0, concat_axis=0, axis_index_groups=[order], tiled=True
    )
    steps = group_bands * xl_all // chunk
    dips = pl.pallas_call(
        lambda *refs: dips_kernel(order, group_bands, xl_part, xl_all, chunk, *refs),
        out_shape=jax.ShapeDtypeStruct((group_bands * 2 * tile_rows * xl_all, NF), jnp.float32),
        in_specs=[vmem],
        out_specs=pl.BlockSpec(memory_space=pltpu.HBM),
        scratch_shapes=[
            pltpu.VMEM((steps, 2 * SUB * chunk, NF), jnp.float32),
            pltpu.VMEM((3, 2 * chunk, 2 * RIM + SUB, NF), jnp.float32),
            pltpu.VMEM((3, group_bands, xl_all + 2 * R, SUB, NF), jnp.float32),
            pltpu.VMEM((2 * NF, 2 * NF), jnp.bfloat16),
            pltpu.SemaphoreType.DMA((steps,)),
        ],
        compiler_params=pltpu.CompilerParams(vmem_limit_bytes=VMEM_LIMIT),
        name="dips",
    )(bricks.reshape(devices * group_bands * xl_part, window, NF))
    return dips.reshape(group_bands, 2, tile_rows, xl_all, NF)


def solution(mesh):
    in_specs = (P(None, ("band", "tile"), None), P())
    out_specs = P("band", None, "tile", None, None)
    return jax.shard_map(local, mesh=mesh, in_specs=in_specs, out_specs=out_specs, check_vma=False)
```

```python
import math

import jax
import jax.numpy as jnp
from jax import lax
from jax.experimental import pallas as pl
from jax.experimental.pallas import tpu as pltpu
from jax.sharding import PartitionSpec as P

NT = 1024
NB = 8
WIN = 64
HOP = 8
SEG = 128
R = 3
NF = 128
SUB = 8
RIM = R + 1

smooth_sigma = 2.0
tiny_value = 1e-06

VMEM_LIMIT = 48 * 1024 * 1024


def stencil_weights():
    weights = [math.exp(-(k * k) / (2.0 * smooth_sigma * smooth_sigma)) for k in range(-R, R + 1)]
    return [weight / sum(weights) for weight in weights]


def turn_sine(turns):
    shifted = (turns + WIN // 4) & (WIN - 1)
    folded = (shifted & (WIN // 2 - 1)) - WIN // 4
    angle = folded.astype(jnp.float32) * (2.0 * math.pi / WIN)
    square = angle * angle
    series = jnp.full_like(angle, -1.0 / 39916800.0)
    for coefficient in (1.0 / 362880.0, -1.0 / 5040.0, 1.0 / 120.0, -1.0 / 6.0, 1.0):
        series = series * square + coefficient
    value = series * angle
    return jnp.where(shifted >= WIN // 2, -value, value)


def turn_cosine(turns):
    return turn_sine(turns + WIN // 4)


def split_halves(value):
    high = value.astype(jnp.bfloat16)
    low = (value - high.astype(jnp.float32)).astype(jnp.bfloat16)
    return high, low


def fill_table(bins_ref, table_ref):
    frames = SEG // HOP
    lane = lax.broadcasted_iota(jnp.int32, (SUB, SEG), 1)
    row = lax.broadcasted_iota(jnp.int32, (SUB, SEG), 0)
    frame, band = lane % frames, lane // frames
    bin_of = jnp.zeros((SUB, SEG), jnp.int32)
    for b in range(NB):
        bin_of = jnp.where(band == b, bins_ref[b], bin_of)
    cosines, sines = [], []
    for group in range(WIN // SUB):
        sample = row + group * SUB
        taper = 0.5 - 0.5 * turn_cosine(sample)
        turns = (bin_of * sample) & (WIN - 1)
        cosines.append(taper * turn_cosine(turns))
        sines.append(-taper * turn_sine(turns))
    zero = jnp.zeros((SUB, SEG), jnp.float32)
    front = WIN // 2 // SUB
    body = SEG // SUB
    tail = (WIN // 2 - HOP) // SUB
    for part, basis in enumerate((cosines, sines)):
        columns = pl.ds(part * SEG, SEG)
        for group in range(front + body + tail):
            value = zero
            for piece in range(WIN // SUB):
                if 0 <= group - piece < frames:
                    value = jnp.where(frame == group - piece, basis[piece], value)
            if group < front:
                at = 2 * body - front + group
            else:
                at = group - front
            table_ref[pl.ds(at * SUB, SUB), columns] = value
        for at in range(body + tail, 2 * body - front):
            table_ref[pl.ds(at * SUB, SUB), columns] = zero


def swap_blocks_and_bands(tiles):
    frames = SEG // HOP
    lane = lax.broadcasted_iota(jnp.int32, (SUB, SEG), 1)
    tiles = list(tiles)
    step = NB // 2
    while step:
        upper = ((lane // frames) & step) != 0
        for at in range(NB):
            if at & step:
                continue
            first, second = tiles[at], tiles[at + step]
            tiles[at] = jnp.where(upper, pltpu.roll(second, frames * step, axis=1), first)
            tiles[at + step] = jnp.where(upper, second, pltpu.roll(first, SEG - frames * step, axis=1))
        step //= 2
    return tiles


def exchange_order(n_band, n_tile):
    count = n_tile // 2
    line = [1, 0, *range(2, count)]
    order = []
    for step in range(2 * n_band):
        last, band = divmod(step ^ (step >> 1), n_band)
        order += [band * n_tile + 2 * line[(at - step) % count] + last for at in range(count)]
    return order


def amplitude_kernel(
    n_band, n_tile, xl_part, far_bins_ref, far_ref, out_ref, table_ref, bins_ref, x_ref, bins_sem, x_sem
):
    bins_copy = pltpu.make_async_copy(far_bins_ref, bins_ref, bins_sem)
    bins_copy.start()
    x_copy = pltpu.make_async_copy(far_ref, x_ref, x_sem)
    x_copy.start()
    bins_copy.wait()
    fill_table(bins_ref, table_ref)
    x_copy.wait()
    table_high, table_low = split_halves(table_ref[...])
    blocks = NT // SEG
    group_bands = NB // n_band
    order = exchange_order(n_band, n_tile)
    pitch = blocks * xl_part
    lane = lax.broadcasted_iota(jnp.int32, (SUB, SEG), 1)
    from_next = lane < WIN // 2 - HOP
    from_last = lane >= SEG - WIN // 2
    zero = jnp.zeros((SUB, SEG), jnp.float32)
    blank = jnp.zeros((RIM, NF), jnp.float32)
    for tile in range(n_tile):
        own, near = [], []
        for xl in range(xl_part):
            line = [
                x_ref[pl.ds(tile * SUB * pitch + block * xl_part + xl, SUB, stride=pitch), :]
                for block in range(blocks)
            ]
            for block in range(blocks):
                later = line[block + 1] if block + 1 < blocks else zero
                earlier = line[block - 1] if block else zero
                near.append(jnp.where(from_next, later, jnp.where(from_last, earlier, zero)))
            own += line
        high, low = split_halves(
            jnp.concatenate([jnp.concatenate(own, 0), jnp.concatenate(near, 0)], 1)
        )
        spectra = jnp.dot(high, table_high, preferred_element_type=jnp.float32)
        spectra += jnp.dot(low, table_high, preferred_element_type=jnp.float32)
        spectra += jnp.dot(high, table_low, preferred_element_type=jnp.float32)
        real_part, imag_part = spectra[:, :SEG], spectra[:, SEG:]
        amplitude = jnp.sqrt(real_part * real_part + imag_part * imag_part)
        for xl in range(xl_part):
            rows = [
                amplitude[(xl * blocks + block) * SUB : (xl * blocks + block + 1) * SUB]
                for block in range(blocks)
            ]
            for band, field in enumerate(swap_blocks_and_bands(rows)):
                group, inner = band // group_bands, band % group_bands

                def place(at):
                    return (order.index(group * n_tile + at) * group_bands + inner) * xl_part + xl

                out_ref[place(tile), RIM : RIM + SUB] = field
                if tile + 1 < n_tile:
                    out_ref[place(tile + 1), :RIM] = field[SUB - RIM :]
                else:
                    out_ref[place(tile), RIM + SUB :] = blank
                if tile:
                    out_ref[place(tile - 1), RIM + SUB :] = field[:RIM]
                else:
                    out_ref[place(tile), :RIM] = blank


def fill_smoother(smoother_ref):
    row = lax.broadcasted_iota(jnp.int32, (NF, NF), 0)
    column = lax.broadcasted_iota(jnp.int32, (NF, NF), 1)
    band_matrix = jnp.zeros((NF, NF), jnp.float32)
    weights = stencil_weights()
    scale = 0.25 * weights[R] * weights[R]
    for k, weight in zip(range(-R, R + 1), weights):
        band_matrix = jnp.where(row - column == k, weight * scale, band_matrix)
    high, low = split_halves(band_matrix)
    smoother_ref[:NF, :NF] = high
    smoother_ref[:NF, NF:] = low
    smoother_ref[NF:, :NF] = high
    smoother_ref[NF:, NF:] = jnp.zeros((NF, NF), jnp.bfloat16)


def weighted(taps):
    weights = stencil_weights()
    total = taps[R]
    for k in range(1, R + 1):
        total += (weights[R + k] / weights[R]) * (taps[R - k] + taps[R + k])
    return total


def dips_kernel(
    order, group_bands, xl_part, xl_all, chunk, e_ref, out_ref, stage_ref, product_ref, row_ref, smoother_ref, sent_ref
):
    fill_smoother(smoother_ref)
    lane = lax.broadcasted_iota(jnp.int32, (SUB, NF), 1)
    at_first, at_last = lane == 0, lane == NF - 1
    zero = jnp.zeros((SUB, NF), jnp.float32)
    low_rows, high_rows = 1, 2 * RIM - 1

    for band in range(group_bands):
        for k in range(R):
            for field in range(3):
                row_ref[field, band, k] = zero
                row_ref[field, band, xl_all + R + k] = zero

    def place(band, xl):
        return order.index(xl // xl_part) * (group_bands * xl_part) + band * xl_part + xl % xl_part

    def shifted_time(value):
        later = jnp.where(at_last, zero, pltpu.roll(value, NF - 1, axis=1))
        return later - jnp.where(at_first, zero, pltpu.roll(value, 1, axis=1))

    def products(band, first):
        lines = []
        for xl in range(first - 1, first + chunk + 1):
            if 0 <= xl < xl_all:
                lines.append([e_ref[place(band, xl), s : s + SUB] for s in (low_rows, high_rows)])
            else:
                lines.append([zero, zero])
        for inner in range(chunk):
            xl = first + inner
            here = place(band, xl)
            slot = xl % (2 * chunk)
            for half, start in enumerate((low_rows, high_rows)):
                value = lines[inner + 1][half]
                grad_il = e_ref[here, start + 1 : start + 1 + SUB] - e_ref[here, start - 1 : start - 1 + SUB]
                grad_xl = lines[inner + 2][half] - lines[inner][half]
                grad_time = shifted_time(value)
                rows = slice(start - low_rows, start - low_rows + SUB)
                product_ref[0, slot, rows] = grad_il * grad_time
                product_ref[1, slot, rows] = grad_xl * grad_time
                product_ref[2, slot, rows] = grad_time * grad_time
            for field in range(3):
                taps = [product_ref[field, slot, k : k + SUB] for k in range(2 * R + 1)]
                row_ref[field, band, xl + R] = weighted(taps)

    def smooth(band, first):
        slot = band * (xl_all // chunk) + first // chunk
        fields = []
        for field in range(3):
            taps = [row_ref[field, band, first + k] for k in range(chunk + 2 * R)]
            for inner in range(chunk):
                fields.append(weighted(taps[inner : inner + 2 * R + 1]))
        high, low = split_halves(jnp.concatenate(fields, 0))
        both = jnp.concatenate([high, low], 1)
        tensor = jnp.dot(both, smoother_ref[...], preferred_element_type=jnp.float32)
        tensor = tensor[:, :NF] + tensor[:, NF:]
        size = chunk * SUB
        inverse = -1.0 / (tensor[2 * size :] + tiny_value)
        for field in range(2):
            dip = tensor[field * size : (field + 1) * size] * inverse
            for inner in range(chunk):
                rows = pl.ds(field * SUB * chunk + inner, SUB, stride=chunk)
                stage_ref[slot, rows, :] = dip[inner * SUB : (inner + 1) * SUB]
        copy = pltpu.make_async_copy(
            stage_ref.at[slot].reshape(2 * SUB, chunk, NF),
            out_ref.at[pl.ds(band * 2 * SUB, 2 * SUB), pl.ds(first, chunk)],
            sent_ref.at[slot],
        )
        copy.start()
        return copy

    copies = []
    for band in range(group_bands):
        for first in range(0, xl_all, chunk):
            products(band, first)
            if first:
                copies.append(smooth(band, first - chunk))
        copies.append(smooth(band, xl_all - chunk))
    for copy in copies:
        copy.wait()


def local(traces, bins):
    n_band = lax.axis_size("band")
    n_tile = lax.axis_size("tile")
    il_all, xl_part, _ = traces.shape
    tile_rows = il_all // n_tile
    group_bands = NB // n_band
    devices = n_band * n_tile
    order = exchange_order(n_band, n_tile)
    xl_all = devices * xl_part
    blocks = NT // SEG
    window = tile_rows + 2 * RIM
    chunk = 8

    lines = traces.reshape(il_all, xl_part, blocks, SEG)
    lines = jnp.transpose(lines, (0, 2, 1, 3)).reshape(il_all * blocks * xl_part, SEG)
    vmem = pl.BlockSpec(memory_space=pltpu.VMEM)
    payload = pl.pallas_call(
        lambda *refs: amplitude_kernel(n_band, n_tile, xl_part, *refs),
        out_shape=jax.ShapeDtypeStruct((devices * group_bands * xl_part, window, NF), jnp.float32),
        in_specs=[pl.BlockSpec(memory_space=pltpu.HBM)] * 2,
        out_specs=vmem,
        scratch_shapes=[
            pltpu.VMEM((2 * SEG, 2 * SEG), jnp.float32),
            pltpu.SMEM(bins.shape, jnp.int32),
            pltpu.VMEM(lines.shape, jnp.float32),
            pltpu.SemaphoreType.DMA,
            pltpu.SemaphoreType.DMA,
        ],
        compiler_params=pltpu.CompilerParams(vmem_limit_bytes=VMEM_LIMIT),
        name="amplitudes",
    )(pltpu.with_memory_space_constraint(bins, pltpu.HBM), pltpu.with_memory_space_constraint(lines, pltpu.HBM))
    payload = payload.reshape(devices, group_bands * xl_part, window, NF)
    bricks = lax.all_to_all(
        payload, ("band", "tile"), split_axis=0, concat_axis=0, axis_index_groups=[order], tiled=True
    )
    steps = group_bands * xl_all // chunk
    dips = pl.pallas_call(
        lambda *refs: dips_kernel(order, group_bands, xl_part, xl_all, chunk, *refs),
        out_shape=jax.ShapeDtypeStruct((group_bands * 2 * tile_rows, xl_all, NF), jnp.float32),
        in_specs=[vmem],
        out_specs=pl.BlockSpec(memory_space=pltpu.HBM),
        scratch_shapes=[
            pltpu.VMEM((steps, 2 * SUB * chunk, NF), jnp.float32),
            pltpu.VMEM((3, 2 * chunk, 2 * RIM + SUB, NF), jnp.float32),
            pltpu.VMEM((3, group_bands, xl_all + 2 * R, SUB, NF), jnp.float32),
            pltpu.VMEM((2 * NF, 2 * NF), jnp.bfloat16),
            pltpu.SemaphoreType.DMA((steps,)),
        ],
        compiler_params=pltpu.CompilerParams(vmem_limit_bytes=VMEM_LIMIT),
        name="dips",
    )(bricks.reshape(devices * group_bands * xl_part, window, NF))
    return dips.reshape(group_bands, 2, tile_rows, xl_all, NF)


def solution(mesh):
    in_specs = (P(None, ("band", "tile"), None), P())
    out_specs = P("band", None, "tile", None, None)
    return jax.shard_map(local, mesh=mesh, in_specs=in_specs, out_specs=out_specs, check_vma=False)
```

```python
import math

import jax
import jax.numpy as jnp
from jax import lax
from jax.experimental import pallas as pl
from jax.experimental.pallas import tpu as pltpu
from jax.sharding import PartitionSpec as P

NT = 1024
NB = 8
WIN = 64
HOP = 8
SEG = 128
R = 3
NF = 128
SUB = 8
RIM = R + 1

smooth_sigma = 2.0
tiny_value = 1e-06

VMEM_LIMIT = 48 * 1024 * 1024


def stencil_weights():
    weights = [math.exp(-(k * k) / (2.0 * smooth_sigma * smooth_sigma)) for k in range(-R, R + 1)]
    return [weight / sum(weights) for weight in weights]


def turn_sine(turns):
    shifted = (turns + WIN // 4) & (WIN - 1)
    folded = (shifted & (WIN // 2 - 1)) - WIN // 4
    angle = folded.astype(jnp.float32) * (2.0 * math.pi / WIN)
    square = angle * angle
    series = jnp.full_like(angle, -1.0 / 39916800.0)
    for coefficient in (1.0 / 362880.0, -1.0 / 5040.0, 1.0 / 120.0, -1.0 / 6.0, 1.0):
        series = series * square + coefficient
    value = series * angle
    return jnp.where(shifted >= WIN // 2, -value, value)


def turn_cosine(turns):
    return turn_sine(turns + WIN // 4)


def split_halves(value):
    high = value.astype(jnp.bfloat16)
    low = (value - high.astype(jnp.float32)).astype(jnp.bfloat16)
    return high, low


def fill_table(bins_ref, table_ref):
    frames = SEG // HOP
    lane = lax.broadcasted_iota(jnp.int32, (SUB, SEG), 1)
    row = lax.broadcasted_iota(jnp.int32, (SUB, SEG), 0)
    frame, band = lane % frames, lane // frames
    bin_of = jnp.zeros((SUB, SEG), jnp.int32)
    for b in range(NB):
        bin_of = jnp.where(band == b, bins_ref[b], bin_of)
    cosines, sines = [], []
    for group in range(WIN // SUB):
        sample = row + group * SUB
        taper = 0.5 - 0.5 * turn_cosine(sample)
        turns = (bin_of * sample) & (WIN - 1)
        cosines.append(taper * turn_cosine(turns))
        sines.append(-taper * turn_sine(turns))
    zero = jnp.zeros((SUB, SEG), jnp.float32)
    front = WIN // 2 // SUB
    body = SEG // SUB
    tail = (WIN // 2 - HOP) // SUB
    for part, basis in enumerate((cosines, sines)):
        columns = pl.ds(part * SEG, SEG)
        for group in range(front + body + tail):
            value = zero
            for piece in range(WIN // SUB):
                if 0 <= group - piece < frames:
                    value = jnp.where(frame == group - piece, basis[piece], value)
            if group < front:
                at = 2 * body - front + group
            else:
                at = group - front
            table_ref[pl.ds(at * SUB, SUB), columns] = value
        for at in range(body + tail, 2 * body - front):
            table_ref[pl.ds(at * SUB, SUB), columns] = zero


def swap_blocks_and_bands(tiles):
    frames = SEG // HOP
    group = lax.broadcasted_iota(jnp.int32, (SUB, SEG), 1) // frames
    tiles = [tiles[0]] + [pltpu.roll(tiles[at], frames * at, axis=1) for at in range(1, NB)]
    step = 1
    while step < NB:
        moved = (group & step) != 0
        tiles = [jnp.where(moved, tiles[(at + step) % NB], tiles[at]) for at in range(NB)]
        step *= 2
    tiles = [tiles[-band % NB] for band in range(NB)]
    return [tiles[0]] + [pltpu.roll(tiles[band], SEG - frames * band, axis=1) for band in range(1, NB)]


def exchange_order(n_band, n_tile):
    count = n_tile // 2
    line = [1, 0, *range(2, count)]
    order = []
    for step in range(2 * n_band):
        last, band = divmod(step ^ (step >> 1), n_band)
        order += [band * n_tile + 2 * line[(at - step) % count] + last for at in range(count)]
    return order


def amplitude_kernel(
    n_band, n_tile, xl_part, far_bins_ref, far_ref, out_ref, table_ref, bins_ref, x_ref, bins_sem, x_sem
):
    bins_copy = pltpu.make_async_copy(far_bins_ref, bins_ref, bins_sem)
    bins_copy.start()
    x_copy = pltpu.make_async_copy(far_ref, x_ref, x_sem)
    x_copy.start()
    bins_copy.wait()
    fill_table(bins_ref, table_ref)
    x_copy.wait()
    table_high, table_low = split_halves(table_ref[...])
    blocks = NT // SEG
    group_bands = NB // n_band
    order = exchange_order(n_band, n_tile)
    pitch = blocks * xl_part
    lane = lax.broadcasted_iota(jnp.int32, (SUB, SEG), 1)
    from_next = lane < WIN // 2 - HOP
    from_last = lane >= SEG - WIN // 2
    zero = jnp.zeros((SUB, SEG), jnp.float32)
    blank = jnp.zeros((RIM, NF), jnp.float32)
    for tile in range(n_tile):
        own, near = [], []
        for xl in range(xl_part):
            line = [
                x_ref[pl.ds(tile * SUB * pitch + block * xl_part + xl, SUB, stride=pitch), :]
                for block in range(blocks)
            ]
            for block in range(blocks):
                later = line[block + 1] if block + 1 < blocks else zero
                earlier = line[block - 1] if block else zero
                near.append(jnp.where(from_next, later, jnp.where(from_last, earlier, zero)))
            own += line
        high, low = split_halves(
            jnp.concatenate([jnp.concatenate(own, 0), jnp.concatenate(near, 0)], 1)
        )
        spectra = jnp.dot(high, table_high, preferred_element_type=jnp.float32)
        spectra += jnp.dot(low, table_high, preferred_element_type=jnp.float32)
        spectra += jnp.dot(high, table_low, preferred_element_type=jnp.float32)
        real_part, imag_part = spectra[:, :SEG], spectra[:, SEG:]
        amplitude = jnp.sqrt(real_part * real_part + imag_part * imag_part)
        for xl in range(xl_part):
            rows = [
                amplitude[(xl * blocks + block) * SUB : (xl * blocks + block + 1) * SUB]
                for block in range(blocks)
            ]
            for band, field in enumerate(swap_blocks_and_bands(rows)):
                group, inner = band // group_bands, band % group_bands

                def place(at):
                    return (order.index(group * n_tile + at) * group_bands + inner) * xl_part + xl

                out_ref[place(tile), RIM : RIM + SUB] = field
                if tile + 1 < n_tile:
                    out_ref[place(tile + 1), :RIM] = field[SUB - RIM :]
                else:
                    out_ref[place(tile), RIM + SUB :] = blank
                if tile:
                    out_ref[place(tile - 1), RIM + SUB :] = field[:RIM]
                else:
                    out_ref[place(tile), :RIM] = blank


def fill_smoother(smoother_ref):
    row = lax.broadcasted_iota(jnp.int32, (NF, NF), 0)
    column = lax.broadcasted_iota(jnp.int32, (NF, NF), 1)
    band_matrix = jnp.zeros((NF, NF), jnp.float32)
    weights = stencil_weights()
    scale = 0.25 * weights[R] * weights[R]
    for k, weight in zip(range(-R, R + 1), weights):
        band_matrix = jnp.where(row - column == k, weight * scale, band_matrix)
    high, low = split_halves(band_matrix)
    smoother_ref[:NF, :NF] = high
    smoother_ref[:NF, NF:] = low
    smoother_ref[NF:, :NF] = high
    smoother_ref[NF:, NF:] = jnp.zeros((NF, NF), jnp.bfloat16)


def weighted(taps):
    weights = stencil_weights()
    total = taps[R]
    for k in range(1, R + 1):
        total += (weights[R + k] / weights[R]) * (taps[R - k] + taps[R + k])
    return total


def dips_kernel(
    order, group_bands, xl_part, xl_all, chunk, e_ref, out_ref, stage_ref, product_ref, row_ref, smoother_ref, sent_ref
):
    fill_smoother(smoother_ref)
    lane = lax.broadcasted_iota(jnp.int32, (SUB, NF), 1)
    at_first, at_last = lane == 0, lane == NF - 1
    zero = jnp.zeros((SUB, NF), jnp.float32)
    low_rows, high_rows = 1, 2 * RIM - 1

    for band in range(group_bands):
        for k in range(R):
            for field in range(3):
                row_ref[field, band, k] = zero
                row_ref[field, band, xl_all + R + k] = zero

    def place(band, xl):
        return order.index(xl // xl_part) * (group_bands * xl_part) + band * xl_part + xl % xl_part

    def shifted_time(value):
        later = jnp.where(at_last, zero, pltpu.roll(value, NF - 1, axis=1))
        return later - jnp.where(at_first, zero, pltpu.roll(value, 1, axis=1))

    def products(band, first):
        lines = []
        for xl in range(first - 1, first + chunk + 1):
            if 0 <= xl < xl_all:
                lines.append([e_ref[place(band, xl), s : s + SUB] for s in (low_rows, high_rows)])
            else:
                lines.append([zero, zero])
        for inner in range(chunk):
            xl = first + inner
            here = place(band, xl)
            slot = band * xl_all + xl
            for half, start in enumerate((low_rows, high_rows)):
                value = lines[inner + 1][half]
                grad_il = e_ref[here, start + 1 : start + 1 + SUB] - e_ref[here, start - 1 : start - 1 + SUB]
                grad_xl = lines[inner + 2][half] - lines[inner][half]
                grad_time = shifted_time(value)
                rows = slice(start - low_rows, start - low_rows + SUB)
                product_ref[0, slot, rows] = grad_il * grad_time
                product_ref[1, slot, rows] = grad_xl * grad_time
                product_ref[2, slot, rows] = grad_time * grad_time
            for field in range(3):
                taps = [product_ref[field, slot, k : k + SUB] for k in range(2 * R + 1)]
                row_ref[field, band, xl + R] = weighted(taps)

    def smooth(band, first):
        slot = band * (xl_all // chunk) + first // chunk
        fields = []
        for field in range(3):
            taps = [row_ref[field, band, first + k] for k in range(chunk + 2 * R)]
            for inner in range(chunk):
                fields.append(weighted(taps[inner : inner + 2 * R + 1]))
        high, low = split_halves(jnp.concatenate(fields, 0))
        both = jnp.concatenate([high, low], 1)
        tensor = jnp.dot(both, smoother_ref[...], preferred_element_type=jnp.float32)
        tensor = tensor[:, :NF] + tensor[:, NF:]
        size = chunk * SUB
        inverse = -1.0 / (tensor[2 * size :] + tiny_value)
        for field in range(2):
            dip = tensor[field * size : (field + 1) * size] * inverse
            for inner in range(chunk):
                rows = pl.ds(field * SUB * chunk + inner, SUB, stride=chunk)
                stage_ref[slot, rows, :] = dip[inner * SUB : (inner + 1) * SUB]
        copy = pltpu.make_async_copy(
            stage_ref.at[slot].reshape(2 * SUB, chunk, NF),
            out_ref.at[pl.ds(band * 2 * SUB, 2 * SUB), pl.ds(first, chunk)],
            sent_ref.at[slot],
        )
        copy.start()
        return copy

    copies = []
    for band in range(group_bands):
        for first in range(0, xl_all, chunk):
            products(band, first)
            if first:
                copies.append(smooth(band, first - chunk))
        copies.append(smooth(band, xl_all - chunk))
    for copy in copies:
        copy.wait()


def local(traces, bins):
    n_band = lax.axis_size("band")
    n_tile = lax.axis_size("tile")
    il_all, xl_part, _ = traces.shape
    tile_rows = il_all // n_tile
    group_bands = NB // n_band
    devices = n_band * n_tile
    order = exchange_order(n_band, n_tile)
    xl_all = devices * xl_part
    blocks = NT // SEG
    window = tile_rows + 2 * RIM
    chunk = 8

    lines = traces.reshape(il_all, xl_part, blocks, SEG)
    lines = jnp.transpose(lines, (0, 2, 1, 3)).reshape(il_all * blocks * xl_part, SEG)
    vmem = pl.BlockSpec(memory_space=pltpu.VMEM)
    payload = pl.pallas_call(
        lambda *refs: amplitude_kernel(n_band, n_tile, xl_part, *refs),
        out_shape=jax.ShapeDtypeStruct((devices * group_bands * xl_part, window, NF), jnp.float32),
        in_specs=[pl.BlockSpec(memory_space=pltpu.HBM)] * 2,
        out_specs=vmem,
        scratch_shapes=[
            pltpu.VMEM((2 * SEG, 2 * SEG), jnp.float32),
            pltpu.SMEM(bins.shape, jnp.int32),
            pltpu.VMEM(lines.shape, jnp.float32),
            pltpu.SemaphoreType.DMA,
            pltpu.SemaphoreType.DMA,
        ],
        compiler_params=pltpu.CompilerParams(vmem_limit_bytes=VMEM_LIMIT),
        name="amplitudes",
    )(pltpu.with_memory_space_constraint(bins, pltpu.HBM), pltpu.with_memory_space_constraint(lines, pltpu.HBM))
    payload = payload.reshape(devices, group_bands * xl_part, window, NF)
    bricks = lax.all_to_all(
        payload, ("band", "tile"), split_axis=0, concat_axis=0, axis_index_groups=[order], tiled=True
    )
    steps = group_bands * xl_all // chunk
    dips = pl.pallas_call(
        lambda *refs: dips_kernel(order, group_bands, xl_part, xl_all, chunk, *refs),
        out_shape=jax.ShapeDtypeStruct((group_bands * 2 * tile_rows, xl_all, NF), jnp.float32),
        in_specs=[vmem],
        out_specs=pl.BlockSpec(memory_space=pltpu.HBM),
        scratch_shapes=[
            pltpu.VMEM((steps, 2 * SUB * chunk, NF), jnp.float32),
            pltpu.VMEM((3, group_bands * xl_all, 2 * RIM + SUB, NF), jnp.float32),
            pltpu.VMEM((3, group_bands, xl_all + 2 * R, SUB, NF), jnp.float32),
            pltpu.VMEM((2 * NF, 2 * NF), jnp.bfloat16),
            pltpu.SemaphoreType.DMA((steps,)),
        ],
        compiler_params=pltpu.CompilerParams(vmem_limit_bytes=VMEM_LIMIT),
        name="dips",
    )(bricks.reshape(devices * group_bands * xl_part, window, NF))
    return dips.reshape(group_bands, 2, tile_rows, xl_all, NF)


def solution(mesh):
    in_specs = (P(None, ("band", "tile"), None), P())
    out_specs = P("band", None, "tile", None, None)
    return jax.shard_map(local, mesh=mesh, in_specs=in_specs, out_specs=out_specs, check_vma=False)
```

```python
import math

import jax
import jax.numpy as jnp
from jax import lax
from jax.experimental import pallas as pl
from jax.experimental.pallas import tpu as pltpu
from jax.sharding import PartitionSpec as P

NT = 1024
NB = 8
WIN = 64
HOP = 8
SEG = 128
R = 3
NF = 128
SUB = 8
RIM = R + 1

smooth_sigma = 2.0
tiny_value = 1e-06

VMEM_LIMIT = 48 * 1024 * 1024


def stencil_weights():
    weights = [math.exp(-(k * k) / (2.0 * smooth_sigma * smooth_sigma)) for k in range(-R, R + 1)]
    return [weight / sum(weights) for weight in weights]


def turn_sine(turns):
    shifted = (turns + WIN // 4) & (WIN - 1)
    folded = (shifted & (WIN // 2 - 1)) - WIN // 4
    angle = folded.astype(jnp.float32) * (2.0 * math.pi / WIN)
    square = angle * angle
    series = jnp.full_like(angle, -1.0 / 39916800.0)
    for coefficient in (1.0 / 362880.0, -1.0 / 5040.0, 1.0 / 120.0, -1.0 / 6.0, 1.0):
        series = series * square + coefficient
    value = series * angle
    return jnp.where(shifted >= WIN // 2, -value, value)


def turn_cosine(turns):
    return turn_sine(turns + WIN // 4)


def split_halves(value):
    high = value.astype(jnp.bfloat16)
    low = (value - high.astype(jnp.float32)).astype(jnp.bfloat16)
    return high, low


def split_parts(value, count):
    parts = []
    for _ in range(count):
        parts.append(value.astype(jnp.bfloat16))
        value = value - parts[-1].astype(jnp.float32)
    return parts


def fill_table(bins_ref, table_ref):
    frames = SEG // HOP
    lane = lax.broadcasted_iota(jnp.int32, (SUB, SEG), 1)
    row = lax.broadcasted_iota(jnp.int32, (SUB, SEG), 0)
    frame, band = lane % frames, lane // frames
    bin_of = jnp.zeros((SUB, SEG), jnp.int32)
    for b in range(NB):
        bin_of = jnp.where(band == b, bins_ref[b], bin_of)
    cosines, sines = [], []
    for group in range(WIN // SUB):
        sample = row + group * SUB
        taper = 0.5 - 0.5 * turn_cosine(sample)
        turns = (bin_of * sample) & (WIN - 1)
        cosines.append(taper * turn_cosine(turns))
        sines.append(-taper * turn_sine(turns))
    zero = jnp.zeros((SUB, SEG), jnp.float32)
    front = WIN // 2 // SUB
    body = SEG // SUB
    tail = (WIN // 2 - HOP) // SUB
    for part, basis in enumerate((cosines, sines)):
        columns = pl.ds(part * SEG, SEG)
        for group in range(front + body + tail):
            value = zero
            for piece in range(WIN // SUB):
                if 0 <= group - piece < frames:
                    value = jnp.where(frame == group - piece, basis[piece], value)
            if group < front:
                at = 2 * body - front + group
            else:
                at = group - front
            table_ref[pl.ds(at * SUB, SUB), columns] = value
        for at in range(body + tail, 2 * body - front):
            table_ref[pl.ds(at * SUB, SUB), columns] = zero


def swap_blocks_and_bands(tiles):
    frames = SEG // HOP
    group = lax.broadcasted_iota(jnp.int32, (SUB, SEG), 1) // frames
    tiles = [tiles[0]] + [pltpu.roll(tiles[at], frames * at, axis=1) for at in range(1, NB)]
    step = 1
    while step < NB:
        moved = (group & step) != 0
        tiles = [jnp.where(moved, tiles[(at + step) % NB], tiles[at]) for at in range(NB)]
        step *= 2
    tiles = [tiles[-band % NB] for band in range(NB)]
    return [tiles[0]] + [pltpu.roll(tiles[band], SEG - frames * band, axis=1) for band in range(1, NB)]


def exchange_order(n_band, n_tile):
    count = n_tile // 2
    line = [1, 0, *range(2, count)]
    order = []
    for step in range(2 * n_band):
        last, band = divmod(step ^ (step >> 1), n_band)
        order += [band * n_tile + 2 * line[(at - step) % count] + last for at in range(count)]
    return order


def amplitude_kernel(
    n_band, n_tile, xl_part, far_bins_ref, far_ref, out_ref, table_ref, bins_ref, x_ref, bins_sem, x_sem
):
    bins_copy = pltpu.make_async_copy(far_bins_ref, bins_ref, bins_sem)
    bins_copy.start()
    x_copy = pltpu.make_async_copy(far_ref, x_ref, x_sem)
    x_copy.start()
    bins_copy.wait()
    fill_table(bins_ref, table_ref)
    x_copy.wait()
    table = split_parts(table_ref[...], 3)
    blocks = NT // SEG
    group_bands = NB // n_band
    order = exchange_order(n_band, n_tile)
    pitch = blocks * xl_part
    lane = lax.broadcasted_iota(jnp.int32, (SUB, SEG), 1)
    from_next = lane < WIN // 2 - HOP
    from_last = lane >= SEG - WIN // 2
    zero = jnp.zeros((SUB, SEG), jnp.float32)
    blank = jnp.zeros((RIM, NF), jnp.float32)
    for tile in range(n_tile):
        own, near = [], []
        for xl in range(xl_part):
            line = [
                x_ref[pl.ds(tile * SUB * pitch + block * xl_part + xl, SUB, stride=pitch), :]
                for block in range(blocks)
            ]
            for block in range(blocks):
                later = line[block + 1] if block + 1 < blocks else zero
                earlier = line[block - 1] if block else zero
                near.append(jnp.where(from_next, later, jnp.where(from_last, earlier, zero)))
            own += line
        samples = split_parts(jnp.concatenate([jnp.concatenate(own, 0), jnp.concatenate(near, 0)], 1), 3)
        spectra = None
        for at in (2, 1, 0):
            count = 3 - at
            term = jnp.dot(jnp.concatenate(samples[:count], 0), table[at], preferred_element_type=jnp.float32)
            size = term.shape[0] // count
            for piece in reversed(range(count)):
                part = term[piece * size : (piece + 1) * size]
                spectra = part if spectra is None else spectra + part
        real_part, imag_part = spectra[:, :SEG], spectra[:, SEG:]
        amplitude = jnp.sqrt(real_part * real_part + imag_part * imag_part)
        for xl in range(xl_part):
            rows = [
                amplitude[(xl * blocks + block) * SUB : (xl * blocks + block + 1) * SUB]
                for block in range(blocks)
            ]
            for band, field in enumerate(swap_blocks_and_bands(rows)):
                group, inner = band // group_bands, band % group_bands

                def place(at):
                    return (order.index(group * n_tile + at) * group_bands + inner) * xl_part + xl

                out_ref[place(tile), RIM : RIM + SUB] = field
                if tile + 1 < n_tile:
                    out_ref[place(tile + 1), :RIM] = field[SUB - RIM :]
                else:
                    out_ref[place(tile), RIM + SUB :] = blank
                if tile:
                    out_ref[place(tile - 1), RIM + SUB :] = field[:RIM]
                else:
                    out_ref[place(tile), :RIM] = blank


def fill_smoother(smoother_ref):
    row = lax.broadcasted_iota(jnp.int32, (NF, NF), 0)
    column = lax.broadcasted_iota(jnp.int32, (NF, NF), 1)
    band_matrix = jnp.zeros((NF, NF), jnp.float32)
    weights = stencil_weights()
    scale = 0.25 * weights[R] * weights[R]
    for k, weight in zip(range(-R, R + 1), weights):
        band_matrix = jnp.where(row - column == k, weight * scale, band_matrix)
    high, low = split_halves(band_matrix)
    smoother_ref[:NF, :NF] = high
    smoother_ref[:NF, NF:] = low
    smoother_ref[NF:, :NF] = high
    smoother_ref[NF:, NF:] = jnp.zeros((NF, NF), jnp.bfloat16)


def weighted(taps):
    weights = stencil_weights()
    total = taps[R]
    for k in range(1, R + 1):
        total += (weights[R + k] / weights[R]) * (taps[R - k] + taps[R + k])
    return total


def dips_kernel(
    order, group_bands, xl_part, xl_all, chunk, e_ref, out_ref, stage_ref, product_ref, row_ref, smoother_ref, sent_ref
):
    fill_smoother(smoother_ref)
    lane = lax.broadcasted_iota(jnp.int32, (SUB, NF), 1)
    at_first, at_last = lane == 0, lane == NF - 1
    zero = jnp.zeros((SUB, NF), jnp.float32)
    low_rows, high_rows = 1, 2 * RIM - 1

    for band in range(group_bands):
        for k in range(R):
            for field in range(3):
                row_ref[field, band, k] = zero
                row_ref[field, band, xl_all + R + k] = zero

    def place(band, xl):
        return order.index(xl // xl_part) * (group_bands * xl_part) + band * xl_part + xl % xl_part

    def shifted_time(value):
        later = jnp.where(at_last, zero, pltpu.roll(value, NF - 1, axis=1))
        return later - jnp.where(at_first, zero, pltpu.roll(value, 1, axis=1))

    def products(band, first):
        lines = []
        for xl in range(first - 1, first + chunk + 1):
            if 0 <= xl < xl_all:
                lines.append([e_ref[place(band, xl), s : s + SUB] for s in (low_rows, high_rows)])
            else:
                lines.append([zero, zero])
        for inner in range(chunk):
            xl = first + inner
            here = place(band, xl)
            slot = band * xl_all + xl
            for half, start in enumerate((low_rows, high_rows)):
                value = lines[inner + 1][half]
                grad_il = e_ref[here, start + 1 : start + 1 + SUB] - e_ref[here, start - 1 : start - 1 + SUB]
                grad_xl = lines[inner + 2][half] - lines[inner][half]
                grad_time = shifted_time(value)
                rows = slice(start - low_rows, start - low_rows + SUB)
                product_ref[0, slot, rows] = grad_il * grad_time
                product_ref[1, slot, rows] = grad_xl * grad_time
                product_ref[2, slot, rows] = grad_time * grad_time
            for field in range(3):
                taps = [product_ref[field, slot, k : k + SUB] for k in range(2 * R + 1)]
                row_ref[field, band, xl + R] = weighted(taps)

    def smooth(band, first):
        slot = band * (xl_all // chunk) + first // chunk
        fields = []
        for field in range(3):
            taps = [row_ref[field, band, first + k] for k in range(chunk + 2 * R)]
            for inner in range(chunk):
                fields.append(weighted(taps[inner : inner + 2 * R + 1]))
        high, low = split_halves(jnp.concatenate(fields, 0))
        both = jnp.concatenate([high, low], 1)
        tensor = jnp.dot(both, smoother_ref[...], preferred_element_type=jnp.float32)
        tensor = tensor[:, :NF] + tensor[:, NF:]
        size = chunk * SUB
        inverse = -1.0 / (tensor[2 * size :] + tiny_value)
        for field in range(2):
            dip = tensor[field * size : (field + 1) * size] * inverse
            for inner in range(chunk):
                rows = pl.ds(field * SUB * chunk + inner, SUB, stride=chunk)
                stage_ref[slot, rows, :] = dip[inner * SUB : (inner + 1) * SUB]
        copy = pltpu.make_async_copy(
            stage_ref.at[slot].reshape(2 * SUB, chunk, NF),
            out_ref.at[pl.ds(band * 2 * SUB, 2 * SUB), pl.ds(first, chunk)],
            sent_ref.at[slot],
        )
        copy.start()
        return copy

    copies = []
    for band in range(group_bands):
        for first in range(0, xl_all, chunk):
            products(band, first)
            if first:
                copies.append(smooth(band, first - chunk))
        copies.append(smooth(band, xl_all - chunk))
    for copy in copies:
        copy.wait()


def local(traces, bins):
    n_band = lax.axis_size("band")
    n_tile = lax.axis_size("tile")
    il_all, xl_part, _ = traces.shape
    tile_rows = il_all // n_tile
    group_bands = NB // n_band
    devices = n_band * n_tile
    order = exchange_order(n_band, n_tile)
    xl_all = devices * xl_part
    blocks = NT // SEG
    window = tile_rows + 2 * RIM
    chunk = 8

    lines = traces.reshape(il_all, xl_part, blocks, SEG)
    lines = jnp.transpose(lines, (0, 2, 1, 3)).reshape(il_all * blocks * xl_part, SEG)
    vmem = pl.BlockSpec(memory_space=pltpu.VMEM)
    payload = pl.pallas_call(
        lambda *refs: amplitude_kernel(n_band, n_tile, xl_part, *refs),
        out_shape=jax.ShapeDtypeStruct((devices * group_bands * xl_part, window, NF), jnp.float32),
        in_specs=[pl.BlockSpec(memory_space=pltpu.HBM)] * 2,
        out_specs=vmem,
        scratch_shapes=[
            pltpu.VMEM((2 * SEG, 2 * SEG), jnp.float32),
            pltpu.SMEM(bins.shape, jnp.int32),
            pltpu.VMEM(lines.shape, jnp.float32),
            pltpu.SemaphoreType.DMA,
            pltpu.SemaphoreType.DMA,
        ],
        compiler_params=pltpu.CompilerParams(vmem_limit_bytes=VMEM_LIMIT),
        name="amplitudes",
    )(pltpu.with_memory_space_constraint(bins, pltpu.HBM), pltpu.with_memory_space_constraint(lines, pltpu.HBM))
    payload = payload.reshape(devices, group_bands * xl_part, window, NF)
    bricks = lax.all_to_all(
        payload, ("band", "tile"), split_axis=0, concat_axis=0, axis_index_groups=[order], tiled=True
    )
    steps = group_bands * xl_all // chunk
    dips = pl.pallas_call(
        lambda *refs: dips_kernel(order, group_bands, xl_part, xl_all, chunk, *refs),
        out_shape=jax.ShapeDtypeStruct((group_bands * 2 * tile_rows, xl_all, NF), jnp.float32),
        in_specs=[vmem],
        out_specs=pl.BlockSpec(memory_space=pltpu.HBM),
        scratch_shapes=[
            pltpu.VMEM((steps, 2 * SUB * chunk, NF), jnp.float32),
            pltpu.VMEM((3, group_bands * xl_all, 2 * RIM + SUB, NF), jnp.float32),
            pltpu.VMEM((3, group_bands, xl_all + 2 * R, SUB, NF), jnp.float32),
            pltpu.VMEM((2 * NF, 2 * NF), jnp.bfloat16),
            pltpu.SemaphoreType.DMA((steps,)),
        ],
        compiler_params=pltpu.CompilerParams(vmem_limit_bytes=VMEM_LIMIT),
        name="dips",
    )(bricks.reshape(devices * group_bands * xl_part, window, NF))
    return dips.reshape(group_bands, 2, tile_rows, xl_all, NF)


def solution(mesh):
    in_specs = (P(None, ("band", "tile"), None), P())
    out_specs = P("band", None, "tile", None, None)
    return jax.shard_map(local, mesh=mesh, in_specs=in_specs, out_specs=out_specs, check_vma=False)
```

```python
import math

import jax
import jax.numpy as jnp
from jax import lax
from jax.experimental import pallas as pl
from jax.experimental.pallas import tpu as pltpu
from jax.sharding import PartitionSpec as P

NT = 1024
NB = 8
WIN = 64
HOP = 8
SEG = 128
R = 3
NF = 128
SUB = 8
RIM = R + 1

smooth_sigma = 2.0
tiny_value = 1e-06

VMEM_LIMIT = 48 * 1024 * 1024


def stencil_weights():
    weights = [math.exp(-(k * k) / (2.0 * smooth_sigma * smooth_sigma)) for k in range(-R, R + 1)]
    return [weight / sum(weights) for weight in weights]


def turn_sine(turns):
    shifted = (turns + WIN // 4) & (WIN - 1)
    folded = (shifted & (WIN // 2 - 1)) - WIN // 4
    angle = folded.astype(jnp.float32) * (2.0 * math.pi / WIN)
    square = angle * angle
    series = jnp.full_like(angle, -1.0 / 39916800.0)
    for coefficient in (1.0 / 362880.0, -1.0 / 5040.0, 1.0 / 120.0, -1.0 / 6.0, 1.0):
        series = series * square + coefficient
    value = series * angle
    return jnp.where(shifted >= WIN // 2, -value, value)


def turn_cosine(turns):
    return turn_sine(turns + WIN // 4)


def split_halves(value):
    high = value.astype(jnp.bfloat16)
    low = (value - high.astype(jnp.float32)).astype(jnp.bfloat16)
    return high, low


def split_parts(value, count):
    parts = []
    for _ in range(count):
        parts.append(value.astype(jnp.bfloat16))
        value = value - parts[-1].astype(jnp.float32)
    return parts


def fill_table(bins_ref, table_ref):
    frames = SEG // HOP
    lane = lax.broadcasted_iota(jnp.int32, (SUB, SEG), 1)
    row = lax.broadcasted_iota(jnp.int32, (SUB, SEG), 0)
    frame, band = lane % frames, lane // frames
    bin_of = jnp.zeros((SUB, SEG), jnp.int32)
    for b in range(NB):
        bin_of = jnp.where(band == b, bins_ref[b], bin_of)
    cosines, sines = [], []
    for group in range(WIN // SUB):
        sample = row + group * SUB
        taper = 0.5 - 0.5 * turn_cosine(sample)
        turns = (bin_of * sample) & (WIN - 1)
        cosines.append(taper * turn_cosine(turns))
        sines.append(-taper * turn_sine(turns))
    zero = jnp.zeros((SUB, SEG), jnp.float32)
    front = WIN // 2 // SUB
    body = SEG // SUB
    tail = (WIN // 2 - HOP) // SUB
    for part, basis in enumerate((cosines, sines)):
        columns = pl.ds(part * SEG, SEG)
        for group in range(front + body + tail):
            value = zero
            for piece in range(WIN // SUB):
                if 0 <= group - piece < frames:
                    value = jnp.where(frame == group - piece, basis[piece], value)
            if group < front:
                at = 2 * body - front + group
            else:
                at = group - front
            table_ref[pl.ds(at * SUB, SUB), columns] = value
        for at in range(body + tail, 2 * body - front):
            table_ref[pl.ds(at * SUB, SUB), columns] = zero


def swap_blocks_and_bands(tiles):
    frames = SEG // HOP
    group = lax.broadcasted_iota(jnp.int32, (SUB, SEG), 1) // frames
    tiles = [tiles[0]] + [pltpu.roll(tiles[at], frames * at, axis=1) for at in range(1, NB)]
    step = 1
    while step < NB:
        moved = (group & step) != 0
        tiles = [jnp.where(moved, tiles[(at + step) % NB], tiles[at]) for at in range(NB)]
        step *= 2
    tiles = [tiles[-band % NB] for band in range(NB)]
    return [tiles[0]] + [pltpu.roll(tiles[band], SEG - frames * band, axis=1) for band in range(1, NB)]


def exchange_order(n_band, n_tile):
    count = n_tile // 2
    line = [1, 2, 0, *range(3, count)]
    turns = (0, 3, 0, 3, 0, 3, 2, 1)
    order = []
    for step in range(2 * n_band):
        last, band = divmod(step ^ (step >> 1), n_band)
        order += [band * n_tile + 2 * line[(at + turns[step % len(turns)]) % count] + last for at in range(count)]
    return order


def amplitude_kernel(
    n_band, n_tile, xl_part, far_bins_ref, far_ref, out_ref, table_ref, bins_ref, x_ref, bins_sem, x_sem
):
    bins_copy = pltpu.make_async_copy(far_bins_ref, bins_ref, bins_sem)
    bins_copy.start()
    x_copy = pltpu.make_async_copy(far_ref, x_ref, x_sem)
    x_copy.start()
    bins_copy.wait()
    fill_table(bins_ref, table_ref)
    table = split_parts(table_ref[...], 3)
    x_copy.wait()
    blocks = NT // SEG
    group_bands = NB // n_band
    order = exchange_order(n_band, n_tile)
    pitch = blocks * xl_part
    lane = lax.broadcasted_iota(jnp.int32, (SUB, SEG), 1)
    from_next = lane < WIN // 2 - HOP
    from_last = lane >= SEG - WIN // 2
    zero = jnp.zeros((SUB, SEG), jnp.float32)
    blank = jnp.zeros((RIM, NF), jnp.float32)
    for tile in range(n_tile):
        own, near = [], []
        for xl in range(xl_part):
            line = [
                x_ref[pl.ds(tile * SUB * pitch + block * xl_part + xl, SUB, stride=pitch), :]
                for block in range(blocks)
            ]
            for block in range(blocks):
                later = line[block + 1] if block + 1 < blocks else zero
                earlier = line[block - 1] if block else zero
                near.append(jnp.where(from_next, later, jnp.where(from_last, earlier, zero)))
            own += line
        samples = split_parts(jnp.concatenate([jnp.concatenate(own, 0), jnp.concatenate(near, 0)], 1), 3)
        spectra = None
        for at in (2, 1, 0):
            count = 3 - at
            term = jnp.dot(jnp.concatenate(samples[:count], 0), table[at], preferred_element_type=jnp.float32)
            size = term.shape[0] // count
            for piece in reversed(range(count)):
                part = term[piece * size : (piece + 1) * size]
                spectra = part if spectra is None else spectra + part
        real_part, imag_part = spectra[:, :SEG], spectra[:, SEG:]
        amplitude = jnp.sqrt(real_part * real_part + imag_part * imag_part)
        for xl in range(xl_part):
            rows = [
                amplitude[(xl * blocks + block) * SUB : (xl * blocks + block + 1) * SUB]
                for block in range(blocks)
            ]
            for band, field in enumerate(swap_blocks_and_bands(rows)):
                group, inner = band // group_bands, band % group_bands

                def place(at):
                    return (order.index(group * n_tile + at) * group_bands + inner) * xl_part + xl

                out_ref[place(tile), RIM : RIM + SUB] = field
                if tile + 1 < n_tile:
                    out_ref[place(tile + 1), :RIM] = field[SUB - RIM :]
                else:
                    out_ref[place(tile), RIM + SUB :] = blank
                if tile:
                    out_ref[place(tile - 1), RIM + SUB :] = field[:RIM]
                else:
                    out_ref[place(tile), :RIM] = blank


def fill_smoother(smoother_ref):
    row = lax.broadcasted_iota(jnp.int32, (NF, NF), 0)
    column = lax.broadcasted_iota(jnp.int32, (NF, NF), 1)
    band_matrix = jnp.zeros((NF, NF), jnp.float32)
    weights = stencil_weights()
    scale = 0.25 * weights[R] * weights[R]
    for k, weight in zip(range(-R, R + 1), weights):
        band_matrix = jnp.where(row - column == k, weight * scale, band_matrix)
    high, low = split_halves(band_matrix)
    smoother_ref[:NF, :NF] = high
    smoother_ref[:NF, NF:] = low
    smoother_ref[NF:, :NF] = high
    smoother_ref[NF:, NF:] = jnp.zeros((NF, NF), jnp.bfloat16)


def weighted(taps):
    weights = stencil_weights()
    total = taps[R]
    for k in range(1, R + 1):
        total += (weights[R + k] / weights[R]) * (taps[R - k] + taps[R + k])
    return total


def dips_kernel(
    order, group_bands, xl_part, xl_all, chunk, e_ref, out_ref, stage_ref, product_ref, row_ref, smoother_ref, sent_ref
):
    fill_smoother(smoother_ref)
    lane = lax.broadcasted_iota(jnp.int32, (SUB, NF), 1)
    at_first, at_last = lane == 0, lane == NF - 1
    zero = jnp.zeros((SUB, NF), jnp.float32)
    low_rows, high_rows = 1, 2 * RIM - 1

    for band in range(group_bands):
        for k in range(R):
            for field in range(3):
                row_ref[field, band, k] = zero
                row_ref[field, band, xl_all + R + k] = zero

    def place(band, xl):
        return order.index(xl // xl_part) * (group_bands * xl_part) + band * xl_part + xl % xl_part

    def shifted_time(value):
        later = jnp.where(at_last, zero, pltpu.roll(value, NF - 1, axis=1))
        return later - jnp.where(at_first, zero, pltpu.roll(value, 1, axis=1))

    def products(band, first):
        lines = []
        for xl in range(first - 1, first + chunk + 1):
            if 0 <= xl < xl_all:
                lines.append([e_ref[place(band, xl), s : s + SUB] for s in (low_rows, high_rows)])
            else:
                lines.append([zero, zero])
        for inner in range(chunk):
            xl = first + inner
            here = place(band, xl)
            slot = band * xl_all + xl
            for half, start in enumerate((low_rows, high_rows)):
                value = lines[inner + 1][half]
                grad_il = e_ref[here, start + 1 : start + 1 + SUB] - e_ref[here, start - 1 : start - 1 + SUB]
                grad_xl = lines[inner + 2][half] - lines[inner][half]
                grad_time = shifted_time(value)
                rows = slice(start - low_rows, start - low_rows + SUB)
                product_ref[0, slot, rows] = grad_il * grad_time
                product_ref[1, slot, rows] = grad_xl * grad_time
                product_ref[2, slot, rows] = grad_time * grad_time
            for field in range(3):
                taps = [product_ref[field, slot, k : k + SUB] for k in range(2 * R + 1)]
                row_ref[field, band, xl + R] = weighted(taps)

    def smooth(band, first):
        slot = band * (xl_all // chunk) + first // chunk
        fields = []
        for field in range(3):
            taps = [row_ref[field, band, first + k] for k in range(chunk + 2 * R)]
            for inner in range(chunk):
                fields.append(weighted(taps[inner : inner + 2 * R + 1]))
        high, low = split_halves(jnp.concatenate(fields, 0))
        both = jnp.concatenate([high, low], 1)
        tensor = jnp.dot(both, smoother_ref[...], preferred_element_type=jnp.float32)
        tensor = tensor[:, :NF] + tensor[:, NF:]
        size = chunk * SUB
        inverse = -1.0 / (tensor[2 * size :] + tiny_value)
        for field in range(2):
            dip = tensor[field * size : (field + 1) * size] * inverse
            for inner in range(chunk):
                rows = pl.ds(field * SUB * chunk + inner, SUB, stride=chunk)
                stage_ref[slot, rows, :] = dip[inner * SUB : (inner + 1) * SUB]
        copy = pltpu.make_async_copy(
            stage_ref.at[slot].reshape(2 * SUB, chunk, NF),
            out_ref.at[pl.ds(band * 2 * SUB, 2 * SUB), pl.ds(first, chunk)],
            sent_ref.at[slot],
        )
        copy.start()
        return copy

    copies = []
    for band in range(group_bands):
        for first in range(0, xl_all, chunk):
            products(band, first)
            if first:
                copies.append(smooth(band, first - chunk))
        copies.append(smooth(band, xl_all - chunk))
    for copy in copies:
        copy.wait()


def local(traces, bins):
    n_band = lax.axis_size("band")
    n_tile = lax.axis_size("tile")
    il_all, xl_part, _ = traces.shape
    tile_rows = il_all // n_tile
    group_bands = NB // n_band
    devices = n_band * n_tile
    order = exchange_order(n_band, n_tile)
    xl_all = devices * xl_part
    blocks = NT // SEG
    window = tile_rows + 2 * RIM
    chunk = 8

    lines = traces.reshape(il_all, xl_part, blocks, SEG)
    lines = jnp.transpose(lines, (0, 2, 1, 3)).reshape(il_all * blocks * xl_part, SEG)
    vmem = pl.BlockSpec(memory_space=pltpu.VMEM)
    payload = pl.pallas_call(
        lambda *refs: amplitude_kernel(n_band, n_tile, xl_part, *refs),
        out_shape=jax.ShapeDtypeStruct((devices * group_bands * xl_part, window, NF), jnp.float32),
        in_specs=[pl.BlockSpec(memory_space=pltpu.HBM)] * 2,
        out_specs=vmem,
        scratch_shapes=[
            pltpu.VMEM((2 * SEG, 2 * SEG), jnp.float32),
            pltpu.SMEM(bins.shape, jnp.int32),
            pltpu.VMEM(lines.shape, jnp.float32),
            pltpu.SemaphoreType.DMA,
            pltpu.SemaphoreType.DMA,
        ],
        compiler_params=pltpu.CompilerParams(vmem_limit_bytes=VMEM_LIMIT),
        name="amplitudes",
    )(pltpu.with_memory_space_constraint(bins, pltpu.HBM), pltpu.with_memory_space_constraint(lines, pltpu.HBM))
    payload = payload.reshape(devices, group_bands * xl_part, window, NF)
    bricks = lax.all_to_all(
        payload, ("band", "tile"), split_axis=0, concat_axis=0, axis_index_groups=[order], tiled=True
    )
    steps = group_bands * xl_all // chunk
    dips = pl.pallas_call(
        lambda *refs: dips_kernel(order, group_bands, xl_part, xl_all, chunk, *refs),
        out_shape=jax.ShapeDtypeStruct((group_bands * 2 * tile_rows, xl_all, NF), jnp.float32),
        in_specs=[vmem],
        out_specs=pl.BlockSpec(memory_space=pltpu.HBM),
        scratch_shapes=[
            pltpu.VMEM((steps, 2 * SUB * chunk, NF), jnp.float32),
            pltpu.VMEM((3, group_bands * xl_all, 2 * RIM + SUB, NF), jnp.float32),
            pltpu.VMEM((3, group_bands, xl_all + 2 * R, SUB, NF), jnp.float32),
            pltpu.VMEM((2 * NF, 2 * NF), jnp.bfloat16),
            pltpu.SemaphoreType.DMA((steps,)),
        ],
        compiler_params=pltpu.CompilerParams(vmem_limit_bytes=VMEM_LIMIT),
        name="dips",
    )(bricks.reshape(devices * group_bands * xl_part, window, NF))
    return dips.reshape(group_bands, 2, tile_rows, xl_all, NF)


def solution(mesh):
    in_specs = (P(None, ("band", "tile"), None), P())
    out_specs = P("band", None, "tile", None, None)
    return jax.shard_map(local, mesh=mesh, in_specs=in_specs, out_specs=out_specs, check_vma=False)
```

```python
import math

import jax
import jax.numpy as jnp
from jax import lax
from jax.experimental import pallas as pl
from jax.experimental.pallas import tpu as pltpu
from jax.sharding import PartitionSpec as P

NT = 1024
NB = 8
WIN = 64
HOP = 8
SEG = 128
R = 3
NF = 128
SUB = 8
RIM = R + 1

smooth_sigma = 2.0
tiny_value = 1e-06

VMEM_LIMIT = 48 * 1024 * 1024


def stencil_weights():
    weights = [math.exp(-(k * k) / (2.0 * smooth_sigma * smooth_sigma)) for k in range(-R, R + 1)]
    return [weight / sum(weights) for weight in weights]


def turn_sine(turns):
    shifted = (turns + WIN // 4) & (WIN - 1)
    folded = (shifted & (WIN // 2 - 1)) - WIN // 4
    angle = folded.astype(jnp.float32) * (2.0 * math.pi / WIN)
    square = angle * angle
    series = jnp.full_like(angle, -1.0 / 39916800.0)
    for coefficient in (1.0 / 362880.0, -1.0 / 5040.0, 1.0 / 120.0, -1.0 / 6.0, 1.0):
        series = series * square + coefficient
    value = series * angle
    return jnp.where(shifted >= WIN // 2, -value, value)


def turn_cosine(turns):
    return turn_sine(turns + WIN // 4)


def split_halves(value):
    high = value.astype(jnp.bfloat16)
    low = (value - high.astype(jnp.float32)).astype(jnp.bfloat16)
    return high, low


def split_parts(value, count):
    parts = []
    for _ in range(count):
        parts.append(value.astype(jnp.bfloat16))
        value = value - parts[-1].astype(jnp.float32)
    return parts


def fill_table(bins_ref, table_ref):
    frames = SEG // HOP
    lane = lax.broadcasted_iota(jnp.int32, (SUB, SEG), 1)
    row = lax.broadcasted_iota(jnp.int32, (SUB, SEG), 0)
    frame, band = lane % frames, lane // frames
    bin_of = jnp.zeros((SUB, SEG), jnp.int32)
    for b in range(NB):
        bin_of = jnp.where(band == b, bins_ref[b], bin_of)
    cosines, sines = [], []
    for group in range(WIN // SUB):
        sample = row + group * SUB
        taper = 0.5 - 0.5 * turn_cosine(sample)
        turns = (bin_of * sample) & (WIN - 1)
        cosines.append(taper * turn_cosine(turns))
        sines.append(-taper * turn_sine(turns))
    zero = jnp.zeros((SUB, SEG), jnp.float32)
    front = WIN // 2 // SUB
    body = SEG // SUB
    tail = (WIN // 2 - HOP) // SUB
    for part, basis in enumerate((cosines, sines)):
        columns = pl.ds(part * SEG, SEG)
        for group in range(front + body + tail):
            value = zero
            for piece in range(WIN // SUB):
                if 0 <= group - piece < frames:
                    value = jnp.where(frame == group - piece, basis[piece], value)
            if group < front:
                at = 2 * body - front + group
            else:
                at = group - front
            table_ref[pl.ds(at * SUB, SUB), columns] = value
        for at in range(body + tail, 2 * body - front):
            table_ref[pl.ds(at * SUB, SUB), columns] = zero


def swap_blocks_and_bands(tiles):
    frames = SEG // HOP
    group = lax.broadcasted_iota(jnp.int32, (SUB, SEG), 1) // frames
    tiles = [tiles[0]] + [pltpu.roll(tiles[at], frames * at, axis=1) for at in range(1, NB)]
    step = 1
    while step < NB:
        moved = (group & step) != 0
        tiles = [jnp.where(moved, tiles[(at + step) % NB], tiles[at]) for at in range(NB)]
        step *= 2
    tiles = [tiles[-band % NB] for band in range(NB)]
    return [tiles[0]] + [pltpu.roll(tiles[band], SEG - frames * band, axis=1) for band in range(1, NB)]


def exchange_order(n_band, n_tile):
    count = n_tile // 2
    line = [1, 2, 0, *range(3, count)]
    turns = (0, 3, 0, 3, 0, 3, 2, 1)
    order = []
    for step in range(2 * n_band):
        last, band = divmod(step ^ (step >> 1), n_band)
        order += [band * n_tile + 2 * line[(at + turns[step % len(turns)]) % count] + last for at in range(count)]
    return order


def amplitude_kernel(
    n_band, n_tile, xl_part, far_bins_ref, far_ref, out_ref, table_ref, bins_ref, x_ref, bins_sem, x_sem
):
    bins_copy = pltpu.make_async_copy(far_bins_ref, bins_ref, bins_sem)
    bins_copy.start()
    x_copy = pltpu.make_async_copy(far_ref, x_ref, x_sem)
    x_copy.start()
    bins_copy.wait()
    fill_table(bins_ref, table_ref)
    table = split_parts(table_ref[...], 3)
    x_copy.wait()
    blocks = NT // SEG
    group_bands = NB // n_band
    order = exchange_order(n_band, n_tile)
    pitch = blocks * xl_part
    lane = lax.broadcasted_iota(jnp.int32, (SUB, SEG), 1)
    from_next = lane < WIN // 2 - HOP
    from_last = lane >= SEG - WIN // 2
    zero = jnp.zeros((SUB, SEG), jnp.float32)
    blank = jnp.zeros((RIM, NF), jnp.float32)
    for first in range(0, n_tile, n_tile):
        own, near = [], []
        for tile in range(first, first + n_tile):
            for xl in range(xl_part):
                line = [
                    x_ref[pl.ds(tile * SUB * pitch + block * xl_part + xl, SUB, stride=pitch), :]
                    for block in range(blocks)
                ]
                for block in range(blocks):
                    later = line[block + 1] if block + 1 < blocks else zero
                    earlier = line[block - 1] if block else zero
                    near.append(jnp.where(from_next, later, jnp.where(from_last, earlier, zero)))
                own += line
        samples = split_parts(jnp.concatenate([jnp.concatenate(own, 0), jnp.concatenate(near, 0)], 1), 3)
        spectra = None
        for at in (2, 1, 0):
            count = 3 - at
            term = jnp.dot(jnp.concatenate(samples[:count], 0), table[at], preferred_element_type=jnp.float32)
            size = term.shape[0] // count
            for piece in reversed(range(count)):
                part = term[piece * size : (piece + 1) * size]
                spectra = part if spectra is None else spectra + part
        real_part, imag_part = spectra[:, :SEG], spectra[:, SEG:]
        amplitude = jnp.sqrt(real_part * real_part + imag_part * imag_part)
        for tile in range(first, first + n_tile):
            for xl in range(xl_part):
                at = ((tile - first) * xl_part + xl) * blocks
                rows = [amplitude[(at + block) * SUB : (at + block + 1) * SUB] for block in range(blocks)]
                for band, field in enumerate(swap_blocks_and_bands(rows)):
                    group, inner = band // group_bands, band % group_bands

                    def place(at):
                        return (order.index(group * n_tile + at) * group_bands + inner) * xl_part + xl

                    out_ref[place(tile), RIM : RIM + SUB] = field
                    if tile + 1 < n_tile:
                        out_ref[place(tile + 1), :RIM] = field[SUB - RIM :]
                    else:
                        out_ref[place(tile), RIM + SUB :] = blank
                    if tile:
                        out_ref[place(tile - 1), RIM + SUB :] = field[:RIM]
                    else:
                        out_ref[place(tile), :RIM] = blank


def fill_smoother(smoother_ref):
    row = lax.broadcasted_iota(jnp.int32, (NF, NF), 0)
    column = lax.broadcasted_iota(jnp.int32, (NF, NF), 1)
    band_matrix = jnp.zeros((NF, NF), jnp.float32)
    weights = stencil_weights()
    scale = 0.25 * weights[R] * weights[R]
    for k, weight in zip(range(-R, R + 1), weights):
        band_matrix = jnp.where(row - column == k, weight * scale, band_matrix)
    high, low = split_halves(band_matrix)
    smoother_ref[:NF, :NF] = high
    smoother_ref[:NF, NF:] = low
    smoother_ref[NF:, :NF] = high
    smoother_ref[NF:, NF:] = jnp.zeros((NF, NF), jnp.bfloat16)


def weighted(taps):
    weights = stencil_weights()
    total = taps[R]
    for k in range(1, R + 1):
        total += (weights[R + k] / weights[R]) * (taps[R - k] + taps[R + k])
    return total


def dips_kernel(
    order, group_bands, xl_part, xl_all, chunk, e_ref, out_ref, stage_ref, product_ref, row_ref, smoother_ref, sent_ref
):
    fill_smoother(smoother_ref)
    lane = lax.broadcasted_iota(jnp.int32, (SUB, NF), 1)
    at_first, at_last = lane == 0, lane == NF - 1
    zero = jnp.zeros((SUB, NF), jnp.float32)
    low_rows, high_rows = 1, 2 * RIM - 1

    for band in range(group_bands):
        for k in range(R):
            for field in range(3):
                row_ref[field, band, k] = zero
                row_ref[field, band, xl_all + R + k] = zero

    def place(band, xl):
        return order.index(xl // xl_part) * (group_bands * xl_part) + band * xl_part + xl % xl_part

    def shifted_time(value):
        later = jnp.where(at_last, zero, pltpu.roll(value, NF - 1, axis=1))
        return later - jnp.where(at_first, zero, pltpu.roll(value, 1, axis=1))

    def products(band, first):
        lines = []
        for xl in range(first - 1, first + chunk + 1):
            if 0 <= xl < xl_all:
                lines.append([e_ref[place(band, xl), s : s + SUB] for s in (low_rows, high_rows)])
            else:
                lines.append([zero, zero])
        for inner in range(chunk):
            xl = first + inner
            here = place(band, xl)
            slot = band * xl_all + xl
            for half, start in enumerate((low_rows, high_rows)):
                value = lines[inner + 1][half]
                grad_il = e_ref[here, start + 1 : start + 1 + SUB] - e_ref[here, start - 1 : start - 1 + SUB]
                grad_xl = lines[inner + 2][half] - lines[inner][half]
                grad_time = shifted_time(value)
                rows = slice(start - low_rows, start - low_rows + SUB)
                product_ref[0, slot, rows] = grad_il * grad_time
                product_ref[1, slot, rows] = grad_xl * grad_time
                product_ref[2, slot, rows] = grad_time * grad_time
            for field in range(3):
                taps = [product_ref[field, slot, k : k + SUB] for k in range(2 * R + 1)]
                row_ref[field, band, xl + R] = weighted(taps)

    def smooth(band, first):
        slot = band * (xl_all // chunk) + first // chunk
        fields = []
        for field in range(3):
            taps = [row_ref[field, band, first + k] for k in range(chunk + 2 * R)]
            for inner in range(chunk):
                fields.append(weighted(taps[inner : inner + 2 * R + 1]))
        high, low = split_halves(jnp.concatenate(fields, 0))
        both = jnp.concatenate([high, low], 1)
        tensor = jnp.dot(both, smoother_ref[...], preferred_element_type=jnp.float32)
        tensor = tensor[:, :NF] + tensor[:, NF:]
        size = chunk * SUB
        inverse = -1.0 / (tensor[2 * size :] + tiny_value)
        for field in range(2):
            dip = tensor[field * size : (field + 1) * size] * inverse
            for inner in range(chunk):
                rows = pl.ds(field * SUB * chunk + inner, SUB, stride=chunk)
                stage_ref[slot, rows, :] = dip[inner * SUB : (inner + 1) * SUB]
        copy = pltpu.make_async_copy(
            stage_ref.at[slot].reshape(2 * SUB, chunk, NF),
            out_ref.at[pl.ds(band * 2 * SUB, 2 * SUB), pl.ds(first, chunk)],
            sent_ref.at[slot],
        )
        copy.start()
        return copy

    copies = []
    for band in range(group_bands):
        for first in range(0, xl_all, chunk):
            products(band, first)
            if first:
                copies.append(smooth(band, first - chunk))
        copies.append(smooth(band, xl_all - chunk))
    for copy in copies:
        copy.wait()


def local(traces, bins):
    n_band = lax.axis_size("band")
    n_tile = lax.axis_size("tile")
    il_all, xl_part, _ = traces.shape
    tile_rows = il_all // n_tile
    group_bands = NB // n_band
    devices = n_band * n_tile
    order = exchange_order(n_band, n_tile)
    xl_all = devices * xl_part
    blocks = NT // SEG
    window = tile_rows + 2 * RIM
    chunk = 8

    lines = traces.reshape(il_all, xl_part, blocks, SEG)
    lines = jnp.transpose(lines, (0, 2, 1, 3)).reshape(il_all * blocks * xl_part, SEG)
    vmem = pl.BlockSpec(memory_space=pltpu.VMEM)
    payload = pl.pallas_call(
        lambda *refs: amplitude_kernel(n_band, n_tile, xl_part, *refs),
        out_shape=jax.ShapeDtypeStruct((devices * group_bands * xl_part, window, NF), jnp.float32),
        in_specs=[pl.BlockSpec(memory_space=pltpu.HBM)] * 2,
        out_specs=vmem,
        scratch_shapes=[
            pltpu.VMEM((2 * SEG, 2 * SEG), jnp.float32),
            pltpu.SMEM(bins.shape, jnp.int32),
            pltpu.VMEM(lines.shape, jnp.float32),
            pltpu.SemaphoreType.DMA,
            pltpu.SemaphoreType.DMA,
        ],
        compiler_params=pltpu.CompilerParams(vmem_limit_bytes=VMEM_LIMIT),
        name="amplitudes",
    )(pltpu.with_memory_space_constraint(bins, pltpu.HBM), pltpu.with_memory_space_constraint(lines, pltpu.HBM))
    payload = payload.reshape(devices, group_bands * xl_part, window, NF)
    bricks = lax.all_to_all(
        payload, ("band", "tile"), split_axis=0, concat_axis=0, axis_index_groups=[order], tiled=True
    )
    steps = group_bands * xl_all // chunk
    dips = pl.pallas_call(
        lambda *refs: dips_kernel(order, group_bands, xl_part, xl_all, chunk, *refs),
        out_shape=jax.ShapeDtypeStruct((group_bands * 2 * tile_rows, xl_all, NF), jnp.float32),
        in_specs=[vmem],
        out_specs=pl.BlockSpec(memory_space=pltpu.HBM),
        scratch_shapes=[
            pltpu.VMEM((steps, 2 * SUB * chunk, NF), jnp.float32),
            pltpu.VMEM((3, group_bands * xl_all, 2 * RIM + SUB, NF), jnp.float32),
            pltpu.VMEM((3, group_bands, xl_all + 2 * R, SUB, NF), jnp.float32),
            pltpu.VMEM((2 * NF, 2 * NF), jnp.bfloat16),
            pltpu.SemaphoreType.DMA((steps,)),
        ],
        compiler_params=pltpu.CompilerParams(vmem_limit_bytes=VMEM_LIMIT),
        name="dips",
    )(bricks.reshape(devices * group_bands * xl_part, window, NF))
    return dips.reshape(group_bands, 2, tile_rows, xl_all, NF)


def solution(mesh):
    in_specs = (P(None, ("band", "tile"), None), P())
    out_specs = P("band", None, "tile", None, None)
    return jax.shard_map(local, mesh=mesh, in_specs=in_specs, out_specs=out_specs, check_vma=False)
```
